32 devices in a mesh: dp: 8 (over y, x, core), tensor: 4 (over z).
Axes of the slice: x: 2, y: 2, z: 4, core: 2. Of those that a mesh axis runs over, the one named last changes fastest.
Arguments:
- hidden: bfloat16 [16, 256, 4096], P('dp', None, 'tensor'), may hold values from -6 to 6
- targets: int32 [16, 256], P('dp'), may hold values from 0 to 511
- lengths: int32 [16], P('dp'), may hold values from 1 to 256, 2048 in all
- conv_filter: bfloat16 [3, 4096], P(None, 'tensor'), may hold values from -3 to 3
- proj_weight: bfloat16 [4096, 4096], P('tensor'), may hold values from -0.09375 to 0.09375
- unembed: bfloat16 [512, 4096], P(None, 'tensor'), may hold values from -0.140625 to 0.140625
- proj_in: bfloat16 [4096, 64], P('tensor'), may hold values from -0.09375 to 0.09375
- proj_out: bfloat16 [4096, 64], P('tensor'), may hold values from -0.09375 to 0.09375
- query_grads: bfloat16 [128, 4096], P('dp', 'tensor'), may hold values from -6 to 6
Outputs:
- scores: float32 [16, 128], P('dp')
The draws below stay inside these ranges and needn't reach their ends.
Inputs may be any that keep to these rules, and one draw needn't show every extreme that they name: `lengths`: some row has exactly 256 live tokens.
All inputs are finite; a program needn't handle non-finite values. No bound on the sum of `lengths` on one device may be relied on, other than what follows from the above.
Results may differ from the reference program's by a relative error of at most 0.0075.
Values may be sent and summed in bfloat16 or wider, within the bound.
No kernel may reach another device: no remote copies, remote signals or barrier semaphores. Data moves between devices by JAX's collectives and lax.ppermute only.
A program may use at most 64 MiB of HBM per device.

```python
import math
import jax
import jax.numpy as jnp
import numpy as np
from jax import lax

D = 4096
VOCAB = 512
RANK = 64
LEN = 256
ROWS = 16
QUERIES = 128


def draw_unembed(key, part):
    key = jax.random.fold_in(key, 11)
    key_shared, key_mixing, key_spread = jax.random.split(key, 3)
    mixing = jax.random.uniform(key_mixing, (VOCAB, 1), jnp.float32, 0.0, 2.0)
    shared = jnp.clip(jax.random.normal(key_shared, (D,), jnp.float32), -3.0, 3.0)
    spread = jnp.clip(jax.random.normal(key_spread, (VOCAB, D), jnp.float32), -3.0, 3.0)
    values = (mixing * shared[None, :] + spread) * (1.0 / math.sqrt(D))
    return values.astype(jnp.bfloat16)


def set_ends(result, stream_key, least, high):
    dims = result.shape
    place = [jax.random.randint(jax.random.fold_in(stream_key, axis), (), 0, dims[axis]) for axis in range(len(dims))]
    result = result.at[tuple(place)].set(least)
    longest = dims.index(max(dims))
    place[longest] = (place[longest] + 1) % dims[longest]
    return result.at[tuple(place)].set(high)


def levels(rng, dims, cuts, low, largest):
    level = 1.0
    for dim, shards_of in cuts:
        steps = jax.random.uniform(jax.random.fold_in(jax.random.fold_in(rng, 6), dim), (shards_of,), jnp.float32, low / len(cuts), largest / len(cuts))
        level = level * jnp.repeat(jnp.exp(steps), dims[dim] // shards_of).reshape((-1,) + (1,) * (len(dims) - 1 - dim))
    return level


def length_profile(amount, total, most, lean):
    loads = [(1 << 20) // math.isqrt(rank ** lean) + 1 for rank in range(2, amount + 1)]
    surplus, counts = total - most - (amount - 1), [1] * (amount - 1)
    while surplus > 0:
        candidates = [i for i in range(amount - 1) if counts[i] < most]
        mass, budget = sum([loads[i] for i in candidates]), surplus
        for i in candidates:
            addition = min(most - counts[i], max(1, budget * loads[i] // mass), surplus)
            counts[i] = counts[i] + addition
            surplus = surplus - addition
    return np.array([most] + counts)


def ragged_sizes(own_key, count, total, bound, skew):
    if count == 2:
        one = jax.random.randint(own_key, (), max(1, total - bound), min(bound, total - 1) + 1)
        return jnp.stack([one, total - one])
    sizes = jnp.asarray(length_profile(count, total, bound, skew), jnp.int32)
    twos = (count - 1) // 2
    giver, receiver = sizes[1:1 + 2 * twos:2], sizes[2:2 + 2 * twos:2]
    room = jnp.minimum(giver - 1, bound - receiver)
    moved = jax.random.randint(jax.random.fold_in(own_key, 1), (twos,), 0, 1 << 20) % (room + 1)
    sizes = sizes.at[1:1 + 2 * twos:2].set(giver - moved).at[2:2 + 2 * twos:2].set(receiver + moved)
    return sizes[jax.random.permutation(jax.random.fold_in(own_key, 2), count)]


def scatter_about(rng, shape, deviation, most, cuts=(), held_as=jnp.bfloat16):
    result = deviation * jax.random.normal(rng, shape, jnp.float32)
    if cuts:
        result = result * levels(rng, shape, cuts, -0.22, 0.18)
    return jnp.clip(result, -most, most).astype(held_as)


def setup_inputs(seed: int = 0) -> dict:
    keys = jax.random.split(jax.random.key(seed), 10)
    return {
        "hidden": scatter_about(keys[0], (ROWS, LEN, D), 1.0, 6.0, ((0, 8), (2, 4))),
        "targets": set_ends(jax.random.randint(keys[1], (ROWS, LEN), 0, VOCAB), jax.random.fold_in(keys[1], 1), 0, VOCAB - 1).astype(jnp.int32),
        "lengths": ragged_sizes(keys[2], ROWS, ROWS * LEN // 2, LEN, 2).astype(jnp.int32),
        "conv_filter": scatter_about(keys[3], (3, D), 0.6, 3.0, ((1, 4),)),
        "proj_weight": scatter_about(keys[4], (D, D), D ** -0.5, 0.09375, ((0, 4),)),
        "unembed": draw_unembed(jax.random.fold_in(keys[9], 71), 0),
        "proj_in": scatter_about(keys[6], (D, RANK), D ** -0.5, 0.09375, ((0, 4),)),
        "proj_out": scatter_about(keys[7], (D, RANK), D ** -0.5, 0.09375, ((0, 4),)),
        "query_grads": scatter_about(keys[8], (QUERIES, RANK * RANK), 1.0, 6.0, ((0, 8), (1, 4))),
    }


eps = 1e-06

def short_conv(hidden, conv_filter):
    values = hidden.astype(jnp.float32)
    taps = conv_filter.astype(jnp.float32)
    zero = jnp.zeros_like(values[..., :1, :])
    first = jnp.concatenate([zero, values[..., :-1, :]], axis=-2)
    second = jnp.concatenate([zero, zero, values[..., :-2, :]], axis=-2)
    return (taps[0] * values + taps[1] * first + taps[2] * second).astype(jnp.bfloat16)

def wide_dot(left, right):
    return jnp.dot(left.astype(jnp.float32), right.astype(jnp.float32), precision=lax.Precision.HIGHEST, preferred_element_type=jnp.float32)

def one_row(item, conv_filter, proj_weight, unembed, proj_in, proj_out):
    row_hidden, row_targets, row_length = item
    mixed = short_conv(row_hidden, conv_filter)
    layer_out = wide_dot(mixed, proj_weight)
    layer_low = layer_out.astype(jnp.bfloat16)
    logits = wide_dot(layer_low, unembed.T)
    expo = jnp.exp(logits)
    prob = expo / lax.optimization_barrier(jnp.sum(expo, axis=1, keepdims=True))
    live = (jnp.arange(LEN) < row_length).astype(jnp.float32)
    onehot = (jnp.arange(VOCAB)[None, :] == row_targets[:, None]).astype(jnp.float32)
    grad_logits = ((prob - onehot) * live[:, None]).astype(jnp.bfloat16)
    grad_out = wide_dot(grad_logits, unembed).astype(jnp.bfloat16)
    side_in = wide_dot(mixed, proj_in)
    side_out = wide_dot(grad_out, proj_out)
    row_grad = wide_dot(side_in.T, side_out).reshape(RANK * RANK)
    row_norm = jnp.sum(row_grad * row_grad)
    return (row_grad.astype(jnp.bfloat16), row_norm)

def reference(hidden, targets, lengths, conv_filter, proj_weight, unembed, proj_in, proj_out, query_grads):
    row_low, row_norm = lax.map(lambda item: one_row(item, conv_filter, proj_weight, unembed, proj_in, proj_out), (hidden, targets, lengths))
    inner = wide_dot(row_low, query_grads.T)
    return inner / jnp.sqrt(row_norm + eps)[:, None]
```

```python
import jax
import jax.numpy as jnp
from jax import lax
from jax.experimental import pallas as pl
from jax.experimental.pallas import tpu as pltpu
from jax.sharding import PartitionSpec as P

eps = 1e-06
f32, bf16 = jnp.float32, jnp.bfloat16
NT = (((1,), (1,)), ((), ()))
TN = (((0,), (0,)), ((), ()))
VM = pl.BlockSpec(memory_space=pltpu.VMEM)
ANY = pl.BlockSpec(memory_space=pl.ANY)
NEAR = [(0, 1), (1, 0), (2, 3), (3, 2)]
FAR = [(0, 2), (3, 1), (1, 0), (2, 3)]


def split2(value, axis):
    high = value.astype(bf16)
    low = (value - high.astype(f32)).astype(bf16)
    return jnp.concatenate([high, low], axis=axis)


def arr(shape, dtype):
    return jax.ShapeDtypeStruct(shape, dtype)


def call(body, outs, args, flops=0, in_specs=None, scratch=()):
    moved = sum(a.size * a.dtype.itemsize for a in args)
    return pl.pallas_call(
        body,
        out_shape=outs,
        in_specs=in_specs or [VM] * len(args),
        out_specs=jax.tree.map(lambda _: VM, outs),
        scratch_shapes=list(scratch),
        cost_estimate=pl.CostEstimate(flops=flops, bytes_accessed=moved, transcendentals=0),
        compiler_params=pltpu.CompilerParams(vmem_limit_bytes=32 << 20),
    )(*args)


def near(x):
    return pltpu.with_memory_space_constraint(x, pltpu.VMEM)


def far(x):
    return pltpu.with_memory_space_constraint(x, pltpu.HBM)


def own_rows(parts, unembed):
    vocab, width = unembed.shape
    step = vocab // parts

    def body(e_ref, out_ref, sem):
        own = pl.multiple_of((lax.axis_index("dp") % parts) * step, step)
        copy = pltpu.make_async_copy(e_ref.at[pl.ds(own, step), :], out_ref, sem)
        copy.start()
        copy.wait()

    return call(
        body,
        arr((step, width), bf16),
        (far(unembed),),
        in_specs=[ANY],
        scratch=[pltpu.SemaphoreType.DMA],
    )


def fold_term(rows, w_ref, share):
    width = rows.shape[1]
    cols = pl.ds(pl.multiple_of(share * width, width), width)
    return lax.dot_general(rows, w_ref[:, cols], NT, preferred_element_type=f32)


def local_work(hidden, conv_filter, proj_in_t, proj_out_t, query_grads, start, proj_weight):
    rows, length, width = hidden.shape
    rank = proj_in_t.shape[0]
    step = start.shape[0]
    tokens = rows * length
    wide = 2 * rank
    q_rows = query_grads.shape[0]
    lines = width // wide
    u_begin = lines * q_rows
    side_begin = u_begin + step

    def body(
        h_any, p_any, o_any, w_any, c_ref, q_ref, b_ref,
        mixed_ref, out_ref, fold_ref, w_ref, h_ref, p_ref, o_ref, hold, sems,
    ):
        pairs = ((h_any, h_ref), (p_any, p_ref), (o_any, o_ref), (w_any, w_ref))
        copies = [pltpu.make_async_copy(a, b, sems.at[k]) for k, (a, b) in enumerate(pairs)]
        for copy in copies:
            copy.start()
        taps = c_ref[...].astype(f32)
        place = lax.broadcasted_iota(jnp.int32, (length, width), 0)
        copies[0].wait()
        for row in range(rows):
            here = h_ref[row].astype(f32)
            first = jnp.where(place >= 1, pltpu.roll(here, 1, 0), 0.0)
            second = jnp.where(place >= 2, pltpu.roll(here, 2, 0), 0.0)
            mixed_ref[pl.ds(row * length, length), :] = (
                taps[0:1] * here + taps[1:2] * first + taps[2:3] * second
            ).astype(bf16)
        copies[1].wait()
        side = lax.dot_general(p_ref[...], mixed_ref[...], NT, preferred_element_type=f32)
        for k in range(tokens // wide):
            hold[k] = side[:, k * wide : (k + 1) * wide]
        for k in range(tokens // wide):
            pair = [hold[k, pl.ds(odd, rank // 2, stride=2), :] for odd in (0, 1)]
            begin = side_begin + k * wide
            out_ref[begin : begin + wide, :] = split2(jnp.concatenate(pair, axis=0), 0)
        for k in range(lines):
            out_ref[k * q_rows : (k + 1) * q_rows, :] = q_ref[:, k * wide : (k + 1) * wide]
        copies[2].wait()
        u = lax.dot_general(b_ref[...], o_ref[...], NT, preferred_element_type=f32)
        out_ref[u_begin:side_begin, :] = split2(u, 1)
        copies[3].wait()
        fold_ref[...] = fold_term(b_ref[...], w_ref, lax.axis_index("tensor"))

    return call(
        body,
        (
            arr((tokens, width), bf16),
            arr((side_begin + tokens, wide), bf16),
            arr((step, width), f32),
            pltpu.VMEM(proj_weight.shape, bf16),
        ),
        (far(hidden), far(proj_in_t), far(proj_out_t), far(proj_weight), conv_filter, query_grads, start),
        2 * tokens * width * rank + 2 * step * width * width,
        in_specs=[ANY] * 4 + [VM] * 3,
        scratch=[
            pltpu.VMEM(hidden.shape, bf16),
            pltpu.VMEM(proj_in_t.shape, bf16),
            pltpu.VMEM(proj_out_t.shape, bf16),
            pltpu.VMEM((tokens // wide, rank, wide), f32),
            pltpu.SemaphoreType.DMA((4,)),
        ],
    )


def fold_more(so_far, block, weight, slot, dtype):
    step, width = block.shape

    def body(f_ref, b_ref, w_ref, out_ref):
        share = lax.axis_index("tensor") ^ slot
        out_ref[...] = (f_ref[...] + fold_term(b_ref[...], w_ref, share)).astype(dtype)

    return call(
        body, arr((step, width), dtype), (so_far, block, near(weight)), 2 * step * width * width
    )


def halve(value):
    half = value.shape[0] // 2
    return value[:half] + value[half:]


def relay_shares(own, near_by, block, step, half):
    wide = own.shape[1]
    begin = block + step
    parts = half // wide

    def body(o_ref, n_ref, out_ref, keep_ref):
        row = lax.axis_index("tensor") // 2
        out_ref[:block, :] = o_ref[:block, :]
        out_ref[block : 2 * block, :] = n_ref[:block, :]
        u = o_ref[block:begin, :].astype(f32) + n_ref[block:begin, :].astype(f32)
        out_ref[2 * block : 2 * block + step, :] = split2(u[:, : wide // 2] + u[:, wide // 2 :], 1)
        for k in range(parts):
            at = [pl.ds(pl.multiple_of(begin + (r * parts + k) * wide, wide // 2), wide) for r in (row, 1 - row)]
            mine, other = [halve(o_ref[c, :].astype(f32) + n_ref[c, :].astype(f32)) for c in at]
            keep_ref[:, k * wide : (k + 1) * wide] = mine
            place = 2 * block + step + k * wide
            out_ref[place : place + wide, :] = split2(other, 0)

    return call(
        body,
        (arr((2 * block + step + half, wide), bf16), arr((wide // 2, half), f32)),
        (own, near_by),
    )


def first_logits(ours, theirs, mixed):
    step, width = ours.shape
    half = mixed.shape[0] // 2

    def body(a_ref, b_ref, m_ref, out_ref):
        weight = jnp.concatenate([a_ref[...], b_ref[...]], axis=0)
        row = 1 - lax.axis_index("tensor") // 2
        tokens = m_ref[pl.ds(pl.multiple_of(row * half, half), half), :]
        logits = lax.dot_general(weight, tokens, NT, preferred_element_type=f32)
        out_ref[...] = logits.astype(bf16)

    return call(
        body, arr((2 * step, half), bf16), (ours, theirs, mixed), 4 * step * half * width
    )


def gather_shares(own, cross, keep, block, step):
    wide = own.shape[1]
    parts = keep.shape[1] // wide
    begin = 2 * block

    def body(o_ref, c_ref, k_ref, out_ref, side_ref):
        me = lax.axis_index("tensor")
        for ref, share in ((o_ref, me), (c_ref, 3 - me)):
            for k, place in enumerate((share, share ^ 1)):
                place = pl.multiple_of(place * block, block)
                out_ref[pl.ds(place, block), :] = ref[k * block : (k + 1) * block, :]
        u = o_ref[begin : begin + step, :].astype(f32) + c_ref[begin : begin + step, :].astype(f32)
        out_ref[4 * block :, :] = split2(u[:, : wide // 2] + u[:, wide // 2 :], 1)
        for k in range(parts):
            cols = slice(k * wide, (k + 1) * wide)
            at = begin + step + k * wide
            side_ref[:, cols] = k_ref[:, cols] + halve(c_ref[at : at + wide, :].astype(f32))

    return call(
        body,
        (arr((4 * block + step, wide), bf16), arr(keep.shape, f32)),
        (own, cross, keep),
        0,
    )


def pass_on(x):
    def body(x_ref, out_ref):
        out_ref[...] = x_ref[...]

    return call(body, arr(x.shape, x.dtype), (x,), 1 << 30)


def stack(pieces):
    high = pieces[0].shape[0]

    def body(*refs):
        for k, ref in enumerate(refs[:-1]):
            refs[-1][k * high : (k + 1) * high, :] = ref[...]

    return call(body, arr((high * len(pieces), pieces[0].shape[1]), bf16), tuple(pieces))


def logit_rows(folded, mixed, *after):
    slots = list(folded)
    step, width = folded[0].shape
    vocab = step * len(folded)
    half = mixed.shape[0] // 2

    def body(*refs):
        parts, refs = refs[: len(folded)], refs[len(folded) :]
        m_ref, (keep_ref, near_ref, other_ref, rest_ref) = refs[0], refs[-4:]
        row = lax.axis_index("tensor") // 2
        weight = jnp.concatenate([parts[slots.index(k)][...] for k in range(len(slots))], axis=0)
        tokens = m_ref[pl.ds(pl.multiple_of((1 - row) * half, half), half), :]
        other = lax.dot_general(weight, tokens, NT, preferred_element_type=f32).astype(bf16)
        other_ref[...] = other
        rest_ref[...] = other[2 * step :]
        tokens = m_ref[pl.ds(pl.multiple_of(row * half, half), half), :]
        mine = lax.dot_general(weight, tokens, NT, preferred_element_type=f32)
        keep_ref[...] = mine
        near_ref[...] = mine.astype(bf16)

    whole = (vocab, half)
    return call(
        body,
        (arr(whole, f32), arr(whole, bf16), arr(whole, bf16), arr((vocab - 2 * step, half), bf16)),
        (*folded.values(), mixed, *after),
        4 * vocab * half * width,
    )


def token_grads(parts, pieces, first, side_in, targets, lengths):
    vocab, length = pieces[0].shape
    rank = side_in.shape[0]
    step = vocab // parts

    def body(k_ref, n_ref, c_ref, f_ref, l_ref, side_ref, t_ref, live_ref, out_ref):
        row = lax.axis_index("tensor") // 2
        own = lax.axis_index("dp") % parts
        total = k_ref[...] + n_ref[...].astype(f32) + c_ref[...].astype(f32)
        total += jnp.concatenate([l_ref[...], f_ref[...]], axis=0).astype(f32)
        expo = jnp.exp(total)
        targets_here = jnp.where(row == 0, t_ref[0:1, :], t_ref[1:2, :])
        lengths_here = jnp.where(row == 0, live_ref[0:1, :], live_ref[1:2, :])
        live = lax.broadcasted_iota(jnp.int32, (1, length), 1) < lengths_here
        scale = jnp.where(live, 1.0 / jnp.sum(expo, axis=0, keepdims=True), 0.0)
        ids = lax.broadcasted_iota(jnp.int32, (vocab, length), 0) ^ (own * step)
        targets_here = jnp.where(live, targets_here, -1)
        grad = (expo * scale - jnp.where(ids == targets_here, 1.0, 0.0)).astype(bf16)
        joint = lax.dot_general(split2(side_ref[...], 0), grad, NT, preferred_element_type=f32)
        out_ref[...] = split2(halve(joint), 0)

    spread = jnp.broadcast_to(lengths[:, None], targets.shape)
    return call(
        body,
        arr((2 * rank, vocab), bf16),
        (*pieces, first, side_in, targets, spread),
        1 << 34,
    )


def row_scores(parts, joint, ours, theirs, queries):
    wide, vocab = joint.shape
    rank = wide // 2
    step = vocab // parts
    lines = rank // 2
    count = parts if queries is None else queries.shape[0]
    high = ours.shape[0] // (parts // 2)
    rows = (high - step) // lines
    extra_args = () if queries is None else (queries,)

    def body(j_ref, a_ref, b_ref, *refs):
        q_ref, refs = (None, refs) if queries is None else (refs[0], refs[1:])
        out_ref, hold = refs
        own = lax.axis_index("dp") % parts
        s_refs = [ref.at[pl.ds(k * high, high), :] for k in range(parts // 2) for ref in (a_ref, b_ref)]
        u = jnp.concatenate([ref[rows * lines :, :] for ref in s_refs], axis=0)
        grads = halve(jnp.dot(j_ref[...], u, preferred_element_type=f32))
        grads = grads[:, :rank] + grads[:, rank:]
        grads = jnp.concatenate([grads[:lines], grads[lines:]], axis=1)
        norm = jnp.sum(grads * grads, keepdims=True)
        low = grads.astype(bf16).astype(f32)
        for k in range(count):
            block = s_refs[k][: rows * lines, :] if q_ref is None else q_ref[k]
            terms = block.astype(f32).reshape(lines, rows, wide) * low[:, None, :]
            place = k if q_ref is not None else k ^ own
            at = pl.ds(pl.multiple_of(place * rows, rows), rows)
            hold[at, :] = split2(jnp.sum(terms, axis=0), 1)
        ones = jnp.ones((16, 2 * wide), bf16)
        inner = lax.dot_general(ones, hold[...], NT, preferred_element_type=f32)
        out_ref[...] = inner[:8] / jnp.sqrt(norm + eps)

    return call(
        body,
        arr((8, count * rows), f32),
        (joint, ours, theirs, *extra_args),
        2 * vocab * rank * rank,
        scratch=[pltpu.VMEM((count * rows, 2 * wide), bf16)],
    )


def join_rows(own, crossed):
    def body(o_ref, c_ref, out_ref):
        first = lax.axis_index("tensor") < 2
        out_ref[0:1] = jnp.where(first, o_ref[0:1], c_ref[0:1])
        out_ref[1:2] = jnp.where(first, c_ref[0:1], o_ref[0:1])

    return call(body, arr(own.shape, f32), (own, crossed))


def pick_rows(joined, came):
    def body(j_ref, c_ref, out_ref):
        me = lax.axis_index("tensor")
        out_ref[...] = jnp.where((me == 1) | (me == 2), j_ref[0:2], c_ref[0:2])

    return call(body, arr((2, joined.shape[1]), f32), (joined, came))


def per_device(
    hidden, targets, lengths, conv_filter, proj_weight, unembed, proj_in, proj_out, query_grads
):
    rows = hidden.shape[0]
    n_dp, n_t = lax.axis_size("dp"), lax.axis_size("tensor")
    assert n_t == 4 and rows == 2
    parts = min(n_dp, 8)

    def send(x, pairs):
        return lax.ppermute(x, "tensor", pairs)

    def cross(x):
        pairs = [(d * 4 + a, e * 4 + b) for d in range(n_dp) for a, e, b in (
            (0, d ^ 1, 0), (1, d, 2), (2, d, 1), (3, d ^ 1, 3))]
        return lax.ppermute(x, ("dp", "tensor"), pairs)

    def swap(x, axis, slot):
        return lax.ppermute(x, axis, [(i, i ^ slot) for i in range(lax.axis_size(axis))])

    start = own_rows(parts, unembed)
    came = {s: swap(start, "tensor", s) for s in (2, 3, 1)}
    mixed, shares, folding, weight = local_work(
        hidden, conv_filter, proj_in.T, proj_out.T, query_grads, start, proj_weight
    )
    shares_near = send(shares, NEAR)
    for s in (2, 1, 3):
        folding = fold_more(folding, came[s], weight, s, bf16 if s == 3 else f32)
    block, step, half = query_grads.size // 128, start.shape[0], hidden.shape[1]
    across, keep_side = relay_shares(shares, shares_near, block, step, half)
    folded = {s: swap(folding, "dp", s) for s in reversed(range(2, parts, 2))}
    folded[0] = folding
    folded |= {s + 1: swap(x, "dp", 1) for s, x in folded.items()}
    first = pass_on(send(first_logits(folded[0], folded[1], mixed), FAR))
    whole, side_in = gather_shares(across, cross(across), keep_side, block, step)
    keep, near_logits, other_logits, rest = logit_rows(folded, mixed, side_in, first)
    pieces = (keep, send(near_logits, NEAR), cross(other_logits), send(rest, FAR))
    queries = None
    if n_dp != parts:
        queries = lax.all_gather(whole[: 4 * block], "dp", axis=0)
    ours = stack([whole] + [swap(whole, "dp", s) for s in range(2, parts, 2)])
    joint = token_grads(parts, pieces, first, side_in, targets, lengths)
    scores = row_scores(parts, joint, ours, swap(ours, "dp", 1), queries)
    joined = join_rows(scores, cross(scores))
    return pick_rows(joined, send(joined, NEAR))


def solution(mesh):
    in_specs = (
        P("dp", None, "tensor"),
        P("dp", None),
        P("dp"),
        P(None, "tensor"),
        P("tensor", None),
        P(None, "tensor"),
        P("tensor", None),
        P("tensor", None),
        P("dp", "tensor"),
    )
    return jax.shard_map(
        per_device, mesh=mesh, in_specs=in_specs, out_specs=P("dp", None), check_vma=False
    )
```

```python
import jax
import jax.numpy as jnp
from jax import lax
from jax.experimental import pallas as pl
from jax.experimental.pallas import tpu as pltpu
from jax.sharding import PartitionSpec as P

eps = 1e-06
f32, bf16 = jnp.float32, jnp.bfloat16
NT = (((1,), (1,)), ((), ()))
TN = (((0,), (0,)), ((), ()))
VM = pl.BlockSpec(memory_space=pltpu.VMEM)
ANY = pl.BlockSpec(memory_space=pl.ANY)
NEAR = [(0, 1), (1, 0), (2, 3), (3, 2)]
FAR = [(0, 2), (3, 1), (1, 0), (2, 3)]


def split2(value, axis):
    high = value.astype(bf16)
    low = (value - high.astype(f32)).astype(bf16)
    return jnp.concatenate([high, low], axis=axis)


def arr(shape, dtype):
    return jax.ShapeDtypeStruct(shape, dtype)


def call(body, outs, args, flops=0, in_specs=None, scratch=()):
    moved = sum(a.size * a.dtype.itemsize for a in args)
    return pl.pallas_call(
        body,
        out_shape=outs,
        in_specs=in_specs or [VM] * len(args),
        out_specs=jax.tree.map(lambda _: VM, outs),
        scratch_shapes=list(scratch),
        cost_estimate=pl.CostEstimate(flops=flops, bytes_accessed=moved, transcendentals=0),
        compiler_params=pltpu.CompilerParams(vmem_limit_bytes=32 << 20),
    )(*args)


def near(x):
    return pltpu.with_memory_space_constraint(x, pltpu.VMEM)


def far(x):
    return pltpu.with_memory_space_constraint(x, pltpu.HBM)


def own_rows(parts, unembed):
    vocab, width = unembed.shape
    step = vocab // parts

    def body(e_ref, out_ref, sem):
        own = pl.multiple_of((lax.axis_index("dp") % parts) * step, step)
        copy = pltpu.make_async_copy(e_ref.at[pl.ds(own, step), :], out_ref, sem)
        copy.start()
        copy.wait()

    return call(
        body,
        arr((step, width), bf16),
        (far(unembed),),
        in_specs=[ANY],
        scratch=[pltpu.SemaphoreType.DMA],
    )


def fold_term(rows, w_ref, share):
    width = rows.shape[1]
    cols = pl.ds(pl.multiple_of(share * width, width), width)
    return lax.dot_general(rows, w_ref[:, cols], NT, preferred_element_type=f32)


def local_work(hidden, conv_filter, proj_in_t, proj_out_t, query_grads, start, proj_weight):
    rows, length, width = hidden.shape
    rank = proj_in_t.shape[0]
    step = start.shape[0]
    tokens = rows * length
    wide = 2 * rank
    q_rows = query_grads.shape[0]
    lines = width // wide
    u_begin = lines * q_rows
    side_begin = u_begin + step

    def body(
        h_any, p_any, o_any, w_any, c_ref, q_ref, b_ref,
        mixed_ref, out_ref, fold_ref, w_ref, h_ref, p_ref, o_ref, hold, sems,
    ):
        pairs = ((h_any, h_ref), (p_any, p_ref), (o_any, o_ref), (w_any, w_ref))
        copies = [pltpu.make_async_copy(a, b, sems.at[k]) for k, (a, b) in enumerate(pairs)]
        for copy in copies:
            copy.start()
        taps = c_ref[...].astype(f32)
        place = lax.broadcasted_iota(jnp.int32, (length, width), 0)
        copies[0].wait()
        for row in range(rows):
            here = h_ref[row].astype(f32)
            first = jnp.where(place >= 1, pltpu.roll(here, 1, 0), 0.0)
            second = jnp.where(place >= 2, pltpu.roll(here, 2, 0), 0.0)
            mixed_ref[pl.ds(row * length, length), :] = (
                taps[0:1] * here + taps[1:2] * first + taps[2:3] * second
            ).astype(bf16)
        copies[1].wait()
        side = lax.dot_general(p_ref[...], mixed_ref[...], NT, preferred_element_type=f32)
        for k in range(tokens // wide):
            hold[k] = side[:, k * wide : (k + 1) * wide]
        for k in range(tokens // wide):
            pair = [hold[k, pl.ds(odd, rank // 2, stride=2), :] for odd in (0, 1)]
            begin = side_begin + k * wide
            out_ref[begin : begin + wide, :] = split2(jnp.concatenate(pair, axis=0), 0)
        for k in range(lines):
            out_ref[k * q_rows : (k + 1) * q_rows, :] = q_ref[:, k * wide : (k + 1) * wide]
        copies[2].wait()
        u = lax.dot_general(b_ref[...], o_ref[...], NT, preferred_element_type=f32)
        out_ref[u_begin:side_begin, :] = split2(u, 1)
        copies[3].wait()
        fold_ref[...] = fold_term(b_ref[...], w_ref, lax.axis_index("tensor"))

    return call(
        body,
        (
            arr((tokens, width), bf16),
            arr((side_begin + tokens, wide), bf16),
            arr((step, width), f32),
            pltpu.VMEM(proj_weight.shape, bf16),
        ),
        (far(hidden), far(proj_in_t), far(proj_out_t), far(proj_weight), conv_filter, query_grads, start),
        2 * tokens * width * rank + 2 * step * width * width,
        in_specs=[ANY] * 4 + [VM] * 3,
        scratch=[
            pltpu.VMEM(hidden.shape, bf16),
            pltpu.VMEM(proj_in_t.shape, bf16),
            pltpu.VMEM(proj_out_t.shape, bf16),
            pltpu.VMEM((tokens // wide, rank, wide), f32),
            pltpu.SemaphoreType.DMA((4,)),
        ],
    )


def fold_more(so_far, block, weight, slot, dtype):
    step, width = block.shape

    def body(f_ref, b_ref, w_ref, out_ref):
        share = lax.axis_index("tensor") ^ slot
        out_ref[...] = (f_ref[...] + fold_term(b_ref[...], w_ref, share)).astype(dtype)

    return call(
        body, arr((step, width), dtype), (so_far, block, near(weight)), 2 * step * width * width
    )


def halve(value):
    half = value.shape[0] // 2
    return value[:half] + value[half:]


def relay_shares(own, near_by, block, step, half):
    wide = own.shape[1]
    begin = block + step
    parts = half // wide

    def body(o_ref, n_ref, out_ref, keep_ref):
        row = lax.axis_index("tensor") // 2
        out_ref[:block, :] = o_ref[:block, :]
        out_ref[block : 2 * block, :] = n_ref[:block, :]
        u = o_ref[block:begin, :].astype(f32) + n_ref[block:begin, :].astype(f32)
        out_ref[2 * block : 2 * block + step, :] = split2(u[:, : wide // 2] + u[:, wide // 2 :], 1)
        for k in range(parts):
            at = [pl.ds(pl.multiple_of(begin + (r * parts + k) * wide, wide // 2), wide) for r in (row, 1 - row)]
            mine, other = [halve(o_ref[c, :].astype(f32) + n_ref[c, :].astype(f32)) for c in at]
            keep_ref[:, k * wide : (k + 1) * wide] = mine
            place = 2 * block + step + k * wide
            out_ref[place : place + wide, :] = split2(other, 0)

    return call(
        body,
        (arr((2 * block + step + half, wide), bf16), arr((wide // 2, half), f32)),
        (own, near_by),
    )


def first_logits(ours, theirs, mixed):
    step, width = ours.shape
    half = mixed.shape[0] // 2

    def body(a_ref, b_ref, m_ref, out_ref):
        weight = jnp.concatenate([a_ref[...], b_ref[...]], axis=0)
        row = 1 - lax.axis_index("tensor") // 2
        tokens = m_ref[pl.ds(pl.multiple_of(row * half, half), half), :]
        logits = lax.dot_general(weight, tokens, NT, preferred_element_type=f32)
        out_ref[...] = logits.astype(bf16)

    return call(
        body, arr((2 * step, half), bf16), (ours, theirs, mixed), 4 * step * half * width
    )


def gather_shares(own, cross, keep, block, step):
    wide = own.shape[1]
    parts = keep.shape[1] // wide
    begin = 2 * block

    def body(o_ref, c_ref, k_ref, out_ref, side_ref):
        me = lax.axis_index("tensor")
        for ref, share in ((o_ref, me), (c_ref, 3 - me)):
            for k, place in enumerate((share, share ^ 1)):
                place = pl.multiple_of(place * block, block)
                out_ref[pl.ds(place, block), :] = ref[k * block : (k + 1) * block, :]
        u = o_ref[begin : begin + step, :].astype(f32) + c_ref[begin : begin + step, :].astype(f32)
        out_ref[4 * block :, :] = split2(u[:, : wide // 2] + u[:, wide // 2 :], 1)
        for k in range(parts):
            cols = slice(k * wide, (k + 1) * wide)
            at = begin + step + k * wide
            side_ref[:, cols] = k_ref[:, cols] + halve(c_ref[at : at + wide, :].astype(f32))

    return call(
        body,
        (arr((4 * block + step, wide), bf16), arr(keep.shape, f32)),
        (own, cross, keep),
        0,
    )


def pass_on(x):
    def body(x_ref, out_ref):
        out_ref[...] = x_ref[...]

    return call(body, arr(x.shape, x.dtype), (x,), 1 << 30)


def stack(pieces):
    high, wide = pieces[0].shape
    places = [slot // 2 * high for slot in pieces]

    def body(*refs):
        for begin, ref in zip(places, refs):
            refs[-1][begin : begin + high, :] = ref[...]

    return call(body, arr((high * len(pieces), wide), bf16), tuple(pieces.values()))


def logit_rows(folded, mixed, *after):
    slots = list(folded)
    step, width = folded[0].shape
    vocab = step * len(folded)
    half = mixed.shape[0] // 2

    def body(*refs):
        parts, refs = refs[: len(folded)], refs[len(folded) :]
        m_ref, (keep_ref, near_ref, other_ref, rest_ref) = refs[0], refs[-4:]
        row = lax.axis_index("tensor") // 2
        weight = jnp.concatenate([parts[slots.index(k)][...] for k in range(len(slots))], axis=0)
        tokens = m_ref[pl.ds(pl.multiple_of((1 - row) * half, half), half), :]
        other = lax.dot_general(weight, tokens, NT, preferred_element_type=f32).astype(bf16)
        other_ref[...] = other
        rest_ref[...] = other[2 * step :]
        tokens = m_ref[pl.ds(pl.multiple_of(row * half, half), half), :]
        mine = lax.dot_general(weight, tokens, NT, preferred_element_type=f32)
        keep_ref[...] = mine
        near_ref[...] = mine.astype(bf16)

    whole = (vocab, half)
    return call(
        body,
        (arr(whole, f32), arr(whole, bf16), arr(whole, bf16), arr((vocab - 2 * step, half), bf16)),
        (*folded.values(), mixed, *after),
        4 * vocab * half * width,
    )


def token_grads(parts, pieces, first, side_in, targets, lengths):
    vocab, length = pieces[0].shape
    rank = side_in.shape[0]
    step = vocab // parts

    def body(k_ref, n_ref, c_ref, f_ref, l_ref, side_ref, t_ref, live_ref, out_ref):
        row = lax.axis_index("tensor") // 2
        own = lax.axis_index("dp") % parts
        total = k_ref[...] + n_ref[...].astype(f32) + c_ref[...].astype(f32)
        total += jnp.concatenate([l_ref[...], f_ref[...]], axis=0).astype(f32)
        expo = jnp.exp(total)
        targets_here = jnp.where(row == 0, t_ref[0:1, :], t_ref[1:2, :])
        lengths_here = jnp.where(row == 0, live_ref[0:1, :], live_ref[1:2, :])
        live = lax.broadcasted_iota(jnp.int32, (1, length), 1) < lengths_here
        scale = jnp.where(live, 1.0 / jnp.sum(expo, axis=0, keepdims=True), 0.0)
        ids = lax.broadcasted_iota(jnp.int32, (vocab, length), 0) ^ (own * step)
        targets_here = jnp.where(live, targets_here, -1)
        grad = (expo * scale - jnp.where(ids == targets_here, 1.0, 0.0)).astype(bf16)
        joint = lax.dot_general(split2(side_ref[...], 0), grad, NT, preferred_element_type=f32)
        out_ref[...] = split2(halve(joint), 0)

    spread = jnp.broadcast_to(lengths[:, None], targets.shape)
    return call(
        body,
        arr((2 * rank, vocab), bf16),
        (*pieces, first, side_in, targets, spread),
        1 << 34,
    )


def row_scores(parts, joint, ours, theirs, queries):
    wide, vocab = joint.shape
    rank = wide // 2
    step = vocab // parts
    lines = rank // 2
    count = parts if queries is None else queries.shape[0]
    high = ours.shape[0] // (parts // 2)
    rows = (high - step) // lines
    extra_args = () if queries is None else (queries,)

    def body(j_ref, a_ref, b_ref, *refs):
        q_ref, refs = (None, refs) if queries is None else (refs[0], refs[1:])
        out_ref, hold = refs
        own = lax.axis_index("dp") % parts
        s_refs = [ref.at[pl.ds(k * high, high), :] for k in range(parts // 2) for ref in (a_ref, b_ref)]
        u = jnp.concatenate([ref[rows * lines :, :] for ref in s_refs], axis=0)
        grads = halve(jnp.dot(j_ref[...], u, preferred_element_type=f32))
        grads = grads[:, :rank] + grads[:, rank:]
        grads = jnp.concatenate([grads[:lines], grads[lines:]], axis=1)
        norm = jnp.sum(grads * grads, keepdims=True)
        low = grads.astype(bf16).astype(f32)
        for k in range(count):
            block = s_refs[k][: rows * lines, :] if q_ref is None else q_ref[k]
            terms = block.astype(f32).reshape(lines, rows, wide) * low[:, None, :]
            place = k if q_ref is not None else k ^ own
            at = pl.ds(pl.multiple_of(place * rows, rows), rows)
            hold[at, :] = split2(jnp.sum(terms, axis=0), 1)
        ones = jnp.ones((16, 2 * wide), bf16)
        inner = lax.dot_general(ones, hold[...], NT, preferred_element_type=f32)
        out_ref[...] = inner[:8] / jnp.sqrt(norm + eps)

    return call(
        body,
        arr((8, count * rows), f32),
        (joint, ours, theirs, *extra_args),
        2 * vocab * rank * rank,
        scratch=[pltpu.VMEM((count * rows, 2 * wide), bf16)],
    )


def join_rows(own, crossed):
    def body(o_ref, c_ref, out_ref):
        first = lax.axis_index("tensor") < 2
        out_ref[0:1] = jnp.where(first, o_ref[0:1], c_ref[0:1])
        out_ref[1:2] = jnp.where(first, c_ref[0:1], o_ref[0:1])

    return call(body, arr(own.shape, f32), (own, crossed))


def pick_rows(joined, came):
    def body(j_ref, c_ref, out_ref):
        me = lax.axis_index("tensor")
        out_ref[...] = jnp.where((me == 1) | (me == 2), j_ref[0:2], c_ref[0:2])

    return call(body, arr((2, joined.shape[1]), f32), (joined, came))


def per_device(
    hidden, targets, lengths, conv_filter, proj_weight, unembed, proj_in, proj_out, query_grads
):
    rows = hidden.shape[0]
    n_dp, n_t = lax.axis_size("dp"), lax.axis_size("tensor")
    assert n_t == 4 and rows == 2
    parts = min(n_dp, 8)

    def send(x, pairs):
        return lax.ppermute(x, "tensor", pairs)

    def cross(x):
        pairs = [(d * 4 + a, e * 4 + b) for d in range(n_dp) for a, e, b in (
            (0, d ^ 1, 0), (1, d, 2), (2, d, 1), (3, d ^ 1, 3))]
        return lax.ppermute(x, ("dp", "tensor"), pairs)

    def swap(x, axis, slot):
        return lax.ppermute(x, axis, [(i, i ^ slot) for i in range(lax.axis_size(axis))])

    start = own_rows(parts, unembed)
    came = {s: swap(start, "tensor", s) for s in (2, 3, 1)}
    mixed, shares, folding, weight = local_work(
        hidden, conv_filter, proj_in.T, proj_out.T, query_grads, start, proj_weight
    )
    shares_near = send(shares, NEAR)
    for s in (2, 1, 3):
        folding = fold_more(folding, came[s], weight, s, bf16 if s == 3 else f32)
    block, step, half = query_grads.size // 128, start.shape[0], hidden.shape[1]
    across, keep_side = relay_shares(shares, shares_near, block, step, half)
    folded = {s: swap(folding, "dp", s) for s in reversed(range(2, parts, 2))}
    folded[0] = folding
    folded |= {s + 1: swap(x, "dp", 1) for s, x in folded.items()}
    first = pass_on(send(first_logits(folded[0], folded[1], mixed), FAR))
    whole, side_in = gather_shares(across, cross(across), keep_side, block, step)
    keep, near_logits, other_logits, rest = logit_rows(folded, mixed, side_in, first)
    pieces = (keep, send(near_logits, NEAR), cross(other_logits), send(rest, FAR))
    queries = None
    if n_dp != parts:
        queries = lax.all_gather(whole[: 4 * block], "dp", axis=0)
    ours = stack({0: whole} | {s: swap(whole, "dp", s) for s in (2, 6, 4)})
    joint = token_grads(parts, pieces, first, side_in, targets, lengths)
    scores = row_scores(parts, joint, ours, swap(ours, "dp", 1), queries)
    joined = join_rows(scores, cross(scores))
    return pick_rows(joined, send(joined, NEAR))


def solution(mesh):
    in_specs = (
        P("dp", None, "tensor"),
        P("dp", None),
        P("dp"),
        P(None, "tensor"),
        P("tensor", None),
        P(None, "tensor"),
        P("tensor", None),
        P("tensor", None),
        P("dp", "tensor"),
    )
    return jax.shard_map(
        per_device, mesh=mesh, in_specs=in_specs, out_specs=P("dp", None), check_vma=False
    )
```

```python
import jax
import jax.numpy as jnp
from jax import lax
from jax.experimental import pallas as pl
from jax.experimental.pallas import tpu as pltpu
from jax.sharding import PartitionSpec as P

eps = 1e-06
f32, bf16 = jnp.float32, jnp.bfloat16
NT = (((1,), (1,)), ((), ()))
TN = (((0,), (0,)), ((), ()))
VM = pl.BlockSpec(memory_space=pltpu.VMEM)
ANY = pl.BlockSpec(memory_space=pl.ANY)
NEAR = [(0, 1), (1, 0), (2, 3), (3, 2)]
FAR = [(0, 2), (3, 1), (1, 0), (2, 3)]


def split2(value, axis):
    high = value.astype(bf16)
    low = (value - high.astype(f32)).astype(bf16)
    return jnp.concatenate([high, low], axis=axis)


def arr(shape, dtype):
    return jax.ShapeDtypeStruct(shape, dtype)


def call(body, outs, args, flops=0, in_specs=None, scratch=()):
    moved = sum(a.size * a.dtype.itemsize for a in args)
    return pl.pallas_call(
        body,
        out_shape=outs,
        in_specs=in_specs or [VM] * len(args),
        out_specs=jax.tree.map(lambda _: VM, outs),
        scratch_shapes=list(scratch),
        cost_estimate=pl.CostEstimate(flops=flops, bytes_accessed=moved, transcendentals=0),
        compiler_params=pltpu.CompilerParams(vmem_limit_bytes=32 << 20),
    )(*args)


def near(x):
    return pltpu.with_memory_space_constraint(x, pltpu.VMEM)


def far(x):
    return pltpu.with_memory_space_constraint(x, pltpu.HBM)


def own_rows(parts, unembed):
    vocab, width = unembed.shape
    step = vocab // parts

    def body(e_ref, out_ref, sem):
        own = pl.multiple_of((lax.axis_index("dp") % parts) * step, step)
        copy = pltpu.make_async_copy(e_ref.at[pl.ds(own, step), :], out_ref, sem)
        copy.start()
        copy.wait()

    return call(
        body,
        arr((step, width), bf16),
        (far(unembed),),
        in_specs=[ANY],
        scratch=[pltpu.SemaphoreType.DMA],
    )


def fold_term(rows, w_ref, share):
    width = rows.shape[1]
    cols = pl.ds(pl.multiple_of(share * width, width), width)
    return lax.dot_general(rows, w_ref[:, cols], NT, preferred_element_type=f32)


def local_work(hidden, conv_filter, proj_in_t, proj_out_t, query_grads, start, proj_weight):
    rows, length, width = hidden.shape
    rank = proj_in_t.shape[0]
    step = start.shape[0]
    tokens = rows * length
    wide = 2 * rank
    q_rows = query_grads.shape[0]
    lines = width // wide
    u_begin = lines * q_rows
    side_begin = u_begin + step

    def body(
        h_any, p_any, o_any, w_any, c_ref, q_ref, b_ref,
        mixed_ref, out_ref, fold_ref, w_ref, h_ref, p_ref, o_ref, hold, sems,
    ):
        pairs = ((h_any, h_ref), (p_any, p_ref), (o_any, o_ref), (w_any, w_ref))
        copies = [pltpu.make_async_copy(a, b, sems.at[k]) for k, (a, b) in enumerate(pairs)]
        for copy in copies:
            copy.start()
        taps = c_ref[...].astype(f32)
        place = lax.broadcasted_iota(jnp.int32, (length, width), 0)
        copies[0].wait()
        for row in range(rows):
            here = h_ref[row].astype(f32)
            first = jnp.where(place >= 1, pltpu.roll(here, 1, 0), 0.0)
            second = jnp.where(place >= 2, pltpu.roll(here, 2, 0), 0.0)
            mixed_ref[pl.ds(row * length, length), :] = (
                taps[0:1] * here + taps[1:2] * first + taps[2:3] * second
            ).astype(bf16)
        copies[1].wait()
        side = lax.dot_general(p_ref[...], mixed_ref[...], NT, preferred_element_type=f32)
        for k in range(tokens // wide):
            hold[k] = side[:, k * wide : (k + 1) * wide]
        for k in range(tokens // wide):
            pair = [hold[k, pl.ds(odd, rank // 2, stride=2), :] for odd in (0, 1)]
            begin = side_begin + k * wide
            out_ref[begin : begin + wide, :] = split2(jnp.concatenate(pair, axis=0), 0)
        for k in range(lines):
            out_ref[k * q_rows : (k + 1) * q_rows, :] = q_ref[:, k * wide : (k + 1) * wide]
        copies[2].wait()
        u = lax.dot_general(b_ref[...], o_ref[...], NT, preferred_element_type=f32)
        out_ref[u_begin:side_begin, :] = split2(u, 1)
        copies[3].wait()
        fold_ref[...] = fold_term(b_ref[...], w_ref, lax.axis_index("tensor"))

    return call(
        body,
        (
            arr((tokens, width), bf16),
            arr((side_begin + tokens, wide), bf16),
            arr((step, width), f32),
            pltpu.VMEM(proj_weight.shape, bf16),
        ),
        (far(hidden), far(proj_in_t), far(proj_out_t), far(proj_weight), conv_filter, query_grads, start),
        2 * tokens * width * rank + 2 * step * width * width,
        in_specs=[ANY] * 4 + [VM] * 3,
        scratch=[
            pltpu.VMEM(hidden.shape, bf16),
            pltpu.VMEM(proj_in_t.shape, bf16),
            pltpu.VMEM(proj_out_t.shape, bf16),
            pltpu.VMEM((tokens // wide, rank, wide), f32),
            pltpu.SemaphoreType.DMA((4,)),
        ],
    )


def fold_more(so_far, block, weight, slot, dtype):
    step, width = block.shape

    def body(f_ref, b_ref, w_ref, out_ref):
        share = lax.axis_index("tensor") ^ slot
        out_ref[...] = (f_ref[...] + fold_term(b_ref[...], w_ref, share)).astype(dtype)

    return call(
        body, arr((step, width), dtype), (so_far, block, near(weight)), 2 * step * width * width
    )


def halve(value):
    half = value.shape[0] // 2
    return value[:half] + value[half:]


def relay_shares(own, near_by, block, step, half):
    wide = own.shape[1]
    begin = block + step
    parts = half // wide

    def body(o_ref, n_ref, out_ref, keep_ref):
        row = lax.axis_index("tensor") // 2
        out_ref[:block, :] = o_ref[:block, :]
        out_ref[block : 2 * block, :] = n_ref[:block, :]
        u = o_ref[block:begin, :].astype(f32) + n_ref[block:begin, :].astype(f32)
        out_ref[2 * block : 2 * block + step, :] = split2(u[:, : wide // 2] + u[:, wide // 2 :], 1)
        for k in range(parts):
            at = [pl.ds(pl.multiple_of(begin + (r * parts + k) * wide, wide // 2), wide) for r in (row, 1 - row)]
            mine, other = [halve(o_ref[c, :].astype(f32) + n_ref[c, :].astype(f32)) for c in at]
            keep_ref[:, k * wide : (k + 1) * wide] = mine
            place = 2 * block + step + k * wide
            out_ref[place : place + wide, :] = split2(other, 0)

    return call(
        body,
        (arr((2 * block + step + half, wide), bf16), arr((wide // 2, half), f32)),
        (own, near_by),
    )


def first_logits(ours, theirs, mixed):
    step, width = ours.shape
    half = mixed.shape[0] // 2

    def body(a_ref, b_ref, m_ref, out_ref):
        weight = jnp.concatenate([a_ref[...], b_ref[...]], axis=0)
        row = 1 - lax.axis_index("tensor") // 2
        tokens = m_ref[pl.ds(pl.multiple_of(row * half, half), half), :]
        logits = lax.dot_general(weight, tokens, NT, preferred_element_type=f32)
        out_ref[...] = logits.astype(bf16)

    return call(
        body, arr((2 * step, half), bf16), (ours, theirs, mixed), 4 * step * half * width
    )


def gather_shares(own, cross, keep, block, step):
    wide = own.shape[1]
    parts = keep.shape[1] // wide
    begin = 2 * block

    def body(o_ref, c_ref, k_ref, out_ref, side_ref):
        me = lax.axis_index("tensor")
        for ref, share in ((o_ref, me), (c_ref, 3 - me)):
            for k, place in enumerate((share, share ^ 1)):
                place = pl.multiple_of(place * block, block)
                out_ref[pl.ds(place, block), :] = ref[k * block : (k + 1) * block, :]
        u = o_ref[begin : begin + step, :].astype(f32) + c_ref[begin : begin + step, :].astype(f32)
        out_ref[4 * block :, :] = split2(u[:, : wide // 2] + u[:, wide // 2 :], 1)
        for k in range(parts):
            cols = slice(k * wide, (k + 1) * wide)
            at = begin + step + k * wide
            side_ref[:, cols] = k_ref[:, cols] + halve(c_ref[at : at + wide, :].astype(f32))

    return call(
        body,
        (arr((4 * block + step, wide), bf16), arr(keep.shape, f32)),
        (own, cross, keep),
        0,
    )


def pass_on(x):
    def body(x_ref, out_ref):
        out_ref[...] = x_ref[...]

    return call(body, arr(x.shape, x.dtype), (x,), 1 << 30)


def stack(pieces):
    high, wide = pieces[0].shape
    places = [slot // 2 * high for slot in pieces]

    def body(*refs):
        for begin, ref in zip(places, refs):
            refs[-1][begin : begin + high, :] = ref[...]

    return call(body, arr((high * len(pieces), wide), bf16), tuple(pieces.values()))


def logit_rows(folded, mixed, *after):
    slots = list(folded)
    step, width = folded[0].shape
    vocab = step * len(folded)
    half = mixed.shape[0] // 2

    def body(*refs):
        parts, refs = refs[: len(folded)], refs[len(folded) :]
        m_ref, (keep_ref, near_ref, other_ref, rest_ref) = refs[0], refs[-4:]
        row = lax.axis_index("tensor") // 2
        weight = jnp.concatenate([parts[slots.index(k)][...] for k in range(len(slots))], axis=0)
        tokens = m_ref[pl.ds(pl.multiple_of((1 - row) * half, half), half), :]
        other = lax.dot_general(weight, tokens, NT, preferred_element_type=f32).astype(bf16)
        other_ref[...] = other
        rest_ref[...] = other[2 * step :]
        tokens = m_ref[pl.ds(pl.multiple_of(row * half, half), half), :]
        mine = lax.dot_general(weight, tokens, NT, preferred_element_type=f32)
        keep_ref[...] = mine
        near_ref[...] = mine.astype(bf16)

    whole = (vocab, half)
    return call(
        body,
        (arr(whole, f32), arr(whole, bf16), arr(whole, bf16), arr((vocab - 2 * step, half), bf16)),
        (*folded.values(), mixed, *after),
        4 * vocab * half * width,
    )


def token_grads(parts, pieces, first, side_in, targets, lengths):
    vocab, length = pieces[0].shape
    rank = side_in.shape[0]
    step = vocab // parts

    def body(k_ref, n_ref, c_ref, f_ref, l_ref, side_ref, t_ref, live_ref, out_ref):
        row = lax.axis_index("tensor") // 2
        own = lax.axis_index("dp") % parts
        total = k_ref[...] + n_ref[...].astype(f32) + c_ref[...].astype(f32)
        total += jnp.concatenate([l_ref[...], f_ref[...]], axis=0).astype(f32)
        expo = jnp.exp(total)
        targets_here = jnp.where(row == 0, t_ref[0:1, :], t_ref[1:2, :])
        lengths_here = jnp.where(row == 0, live_ref[0:1, :], live_ref[1:2, :])
        live = lax.broadcasted_iota(jnp.int32, (1, length), 1) < lengths_here
        scale = jnp.where(live, 1.0 / jnp.sum(expo, axis=0, keepdims=True), 0.0)
        ids = lax.broadcasted_iota(jnp.int32, (vocab, length), 0) ^ (own * step)
        targets_here = jnp.where(live, targets_here, -1)
        grad = (expo * scale - jnp.where(ids == targets_here, 1.0, 0.0)).astype(bf16)
        joint = lax.dot_general(split2(side_ref[...], 0), grad, NT, preferred_element_type=f32)
        out_ref[...] = split2(halve(joint), 0)

    spread = jnp.broadcast_to(lengths[:, None], targets.shape)
    return call(
        body,
        arr((2 * rank, vocab), bf16),
        (*pieces, first, side_in, targets, spread),
        1 << 34,
    )


def row_scores(parts, joint, ours, theirs, queries):
    wide, vocab = joint.shape
    rank = wide // 2
    step = vocab // parts
    lines = rank // 2
    count = parts if queries is None else queries.shape[0]
    high = ours.shape[0] // (parts // 2)
    rows = (high - step) // lines
    extra_args = () if queries is None else (queries,)

    def body(j_ref, a_ref, b_ref, *refs):
        q_ref, refs = (None, refs) if queries is None else (refs[0], refs[1:])
        out_ref, hold = refs
        own = lax.axis_index("dp") % parts
        s_refs = [ref.at[pl.ds(k * high, high), :] for k in range(parts // 2) for ref in (a_ref, b_ref)]
        u = jnp.concatenate([ref[rows * lines :, :] for ref in s_refs], axis=0)
        grads = halve(jnp.dot(j_ref[...], u, preferred_element_type=f32))
        grads = grads[:, :rank] + grads[:, rank:]
        grads = jnp.concatenate([grads[:lines], grads[lines:]], axis=1)
        norm = jnp.sum(grads * grads, keepdims=True)
        low = grads.astype(bf16).astype(f32)
        for k in range(count):
            block = s_refs[k][: rows * lines, :] if q_ref is None else q_ref[k]
            terms = block.astype(f32).reshape(lines, rows, wide) * low[:, None, :]
            place = k if q_ref is not None else k ^ own
            at = pl.ds(pl.multiple_of(place * rows, rows), rows)
            hold[at, :] = split2(jnp.sum(terms, axis=0), 1)
        ones = jnp.ones((16, 2 * wide), bf16)
        inner = lax.dot_general(ones, hold[...], NT, preferred_element_type=f32)
        out_ref[...] = inner[:8] / jnp.sqrt(norm + eps)

    return call(
        body,
        arr((8, count * rows), f32),
        (joint, ours, theirs, *extra_args),
        2 * vocab * rank * rank,
        scratch=[pltpu.VMEM((count * rows, 2 * wide), bf16)],
    )


def join_rows(own, crossed):
    def body(o_ref, c_ref, out_ref):
        first = lax.axis_index("tensor") < 2
        out_ref[0:1] = jnp.where(first, o_ref[0:1], c_ref[0:1])
        out_ref[1:2] = jnp.where(first, c_ref[0:1], o_ref[0:1])

    return call(body, arr(own.shape, f32), (own, crossed))


def pick_rows(joined, came):
    def body(j_ref, c_ref, out_ref):
        me = lax.axis_index("tensor")
        out_ref[...] = jnp.where((me == 1) | (me == 2), j_ref[0:2], c_ref[0:2])

    return call(body, arr((2, joined.shape[1]), f32), (joined, came))


def per_device(
    hidden, targets, lengths, conv_filter, proj_weight, unembed, proj_in, proj_out, query_grads
):
    rows = hidden.shape[0]
    n_dp, n_t = lax.axis_size("dp"), lax.axis_size("tensor")
    assert n_t == 4 and rows == 2
    parts = min(n_dp, 8)

    def send(x, pairs):
        return lax.ppermute(x, "tensor", pairs)

    def cross(x):
        pairs = [(d * 4 + a, e * 4 + b) for d in range(n_dp) for a, e, b in (
            (0, d ^ 1, 0), (1, d, 2), (2, d, 1), (3, d ^ 1, 3))]
        return lax.ppermute(x, ("dp", "tensor"), pairs)

    def swap(x, axis, slot):
        return lax.ppermute(x, axis, [(i, i ^ slot) for i in range(lax.axis_size(axis))])

    start = own_rows(parts, unembed)
    came = {s: swap(start, "tensor", s) for s in (2, 3, 1)}
    mixed, shares, folding, weight = local_work(
        hidden, conv_filter, proj_in.T, proj_out.T, query_grads, start, proj_weight
    )
    shares_near = send(shares, NEAR)
    for s in (2, 1, 3):
        folding = fold_more(folding, came[s], weight, s, bf16 if s == 3 else f32)
    block, step, half = query_grads.size // 128, start.shape[0], hidden.shape[1]
    across, keep_side = relay_shares(shares, shares_near, block, step, half)
    folded = {s: swap(folding, "dp", s) for s in reversed(range(2, parts, 2))}
    folded[0] = folding
    folded |= {s + 1: swap(x, "dp", 1) for s, x in folded.items()}
    first = pass_on(send(first_logits(folded[0], folded[1], mixed), FAR))
    whole, side_in = gather_shares(across, cross(across), keep_side, block, step)
    keep, near_logits, other_logits, rest = logit_rows(folded, mixed, side_in, first)
    pieces = (keep, send(near_logits, NEAR), cross(other_logits), send(rest, FAR))
    queries = None
    if n_dp != parts:
        queries = lax.all_gather(whole[: 4 * block], "dp", axis=0)
    ours = stack({0: whole} | {s: swap(whole, "dp", s) for s in (4, 6, 2)})
    joint = token_grads(parts, pieces, first, side_in, targets, lengths)
    scores = row_scores(parts, joint, ours, swap(ours, "dp", 1), queries)
    joined = join_rows(scores, cross(scores))
    return pick_rows(joined, send(joined, NEAR))


def solution(mesh):
    in_specs = (
        P("dp", None, "tensor"),
        P("dp", None),
        P("dp"),
        P(None, "tensor"),
        P("tensor", None),
        P(None, "tensor"),
        P("tensor", None),
        P("tensor", None),
        P("dp", "tensor"),
    )
    return jax.shard_map(
        per_device, mesh=mesh, in_specs=in_specs, out_specs=P("dp", None), check_vma=False
    )
```

```python
import jax
import jax.numpy as jnp
from jax import lax
from jax.experimental import pallas as pl
from jax.experimental.pallas import tpu as pltpu
from jax.sharding import PartitionSpec as P

eps = 1e-06
f32, bf16 = jnp.float32, jnp.bfloat16
NT = (((1,), (1,)), ((), ()))
TN = (((0,), (0,)), ((), ()))
VM = pl.BlockSpec(memory_space=pltpu.VMEM)
ANY = pl.BlockSpec(memory_space=pl.ANY)
NEAR = [(0, 1), (1, 0), (2, 3), (3, 2)]
FAR = [(0, 2), (3, 1), (1, 0), (2, 3)]


def split2(value, axis):
    high = value.astype(bf16)
    low = (value - high.astype(f32)).astype(bf16)
    return jnp.concatenate([high, low], axis=axis)


def arr(shape, dtype):
    return jax.ShapeDtypeStruct(shape, dtype)


def call(body, outs, args, flops=0, in_specs=None, scratch=()):
    moved = sum(a.size * a.dtype.itemsize for a in args)
    return pl.pallas_call(
        body,
        out_shape=outs,
        in_specs=in_specs or [VM] * len(args),
        out_specs=jax.tree.map(lambda _: VM, outs),
        scratch_shapes=list(scratch),
        cost_estimate=pl.CostEstimate(flops=flops, bytes_accessed=moved, transcendentals=0),
        compiler_params=pltpu.CompilerParams(vmem_limit_bytes=32 << 20),
    )(*args)


def near(x):
    return pltpu.with_memory_space_constraint(x, pltpu.VMEM)


def far(x):
    return pltpu.with_memory_space_constraint(x, pltpu.HBM)


def own_rows(parts, unembed):
    vocab, width = unembed.shape
    step = vocab // parts

    def body(e_ref, out_ref, sem):
        own = pl.multiple_of((lax.axis_index("dp") % parts) * step, step)
        copy = pltpu.make_async_copy(e_ref.at[pl.ds(own, step), :], out_ref, sem)
        copy.start()
        copy.wait()

    return call(
        body,
        arr((step, width), bf16),
        (far(unembed),),
        in_specs=[ANY],
        scratch=[pltpu.SemaphoreType.DMA],
    )


def fold_term(rows, w_ref, share):
    width = rows.shape[1]
    cols = pl.ds(pl.multiple_of(share * width, width), width)
    return lax.dot_general(rows, w_ref[:, cols], NT, preferred_element_type=f32)


def local_work(hidden, conv_filter, proj_in_t, proj_out_t, query_grads, start, proj_weight):
    rows, length, width = hidden.shape
    rank = proj_in_t.shape[0]
    step = start.shape[0]
    tokens = rows * length
    wide = 2 * rank
    q_rows = query_grads.shape[0]
    lines = width // wide
    u_begin = lines * q_rows
    side_begin = u_begin + step

    def body(
        h_any, p_any, o_any, w_any, c_ref, q_ref, b_ref,
        mixed_ref, out_ref, fold_ref, w_ref, h_ref, p_ref, o_ref, hold, sems,
    ):
        pairs = ((h_any, h_ref), (p_any, p_ref), (o_any, o_ref), (w_any, w_ref))
        copies = [pltpu.make_async_copy(a, b, sems.at[k]) for k, (a, b) in enumerate(pairs)]
        for copy in copies:
            copy.start()
        taps = c_ref[...].astype(f32)
        place = lax.broadcasted_iota(jnp.int32, (length, width), 0)
        copies[0].wait()
        for row in range(rows):
            here = h_ref[row].astype(f32)
            first = jnp.where(place >= 1, pltpu.roll(here, 1, 0), 0.0)
            second = jnp.where(place >= 2, pltpu.roll(here, 2, 0), 0.0)
            mixed_ref[pl.ds(row * length, length), :] = (
                taps[0:1] * here + taps[1:2] * first + taps[2:3] * second
            ).astype(bf16)
        copies[1].wait()
        side = lax.dot_general(p_ref[...], mixed_ref[...], NT, preferred_element_type=f32)
        for k in range(tokens // wide):
            hold[k] = side[:, k * wide : (k + 1) * wide]
        for k in range(tokens // wide):
            pair = [hold[k, pl.ds(odd, rank // 2, stride=2), :] for odd in (0, 1)]
            begin = side_begin + k * wide
            out_ref[begin : begin + wide, :] = split2(jnp.concatenate(pair, axis=0), 0)
        for k in range(lines):
            out_ref[k * q_rows : (k + 1) * q_rows, :] = q_ref[:, k * wide : (k + 1) * wide]
        copies[2].wait()
        u = lax.dot_general(b_ref[...], o_ref[...], NT, preferred_element_type=f32)
        out_ref[u_begin:side_begin, :] = split2(u, 1)
        copies[3].wait()
        fold_ref[...] = fold_term(b_ref[...], w_ref, lax.axis_index("tensor"))

    return call(
        body,
        (
            arr((tokens, width), bf16),
            arr((side_begin + tokens, wide), bf16),
            arr((step, width), f32),
            pltpu.VMEM(proj_weight.shape, bf16),
        ),
        (far(hidden), far(proj_in_t), far(proj_out_t), far(proj_weight), conv_filter, query_grads, start),
        2 * tokens * width * rank + 2 * step * width * width,
        in_specs=[ANY] * 4 + [VM] * 3,
        scratch=[
            pltpu.VMEM(hidden.shape, bf16),
            pltpu.VMEM(proj_in_t.shape, bf16),
            pltpu.VMEM(proj_out_t.shape, bf16),
            pltpu.VMEM((tokens // wide, rank, wide), f32),
            pltpu.SemaphoreType.DMA((4,)),
        ],
    )


def fold_more(so_far, block, weight, slot, dtype):
    step, width = block.shape

    def body(f_ref, b_ref, w_ref, out_ref):
        share = lax.axis_index("tensor") ^ slot
        out_ref[...] = (f_ref[...] + fold_term(b_ref[...], w_ref, share)).astype(dtype)

    return call(
        body, arr((step, width), dtype), (so_far, block, near(weight)), 2 * step * width * width
    )


def halve(value):
    half = value.shape[0] // 2
    return value[:half] + value[half:]


def relay_shares(own, near_by, block, step, half):
    wide = own.shape[1]
    begin = block + step
    parts = half // wide

    def body(o_ref, n_ref, out_ref, keep_ref):
        row = lax.axis_index("tensor") // 2
        out_ref[:block, :] = o_ref[:block, :]
        out_ref[block : 2 * block, :] = n_ref[:block, :]
        u = o_ref[block:begin, :].astype(f32) + n_ref[block:begin, :].astype(f32)
        out_ref[2 * block : 2 * block + step, :] = split2(u[:, : wide // 2] + u[:, wide // 2 :], 1)
        for k in range(parts):
            at = [pl.ds(pl.multiple_of(begin + (r * parts + k) * wide, wide // 2), wide) for r in (row, 1 - row)]
            mine, other = [halve(o_ref[c, :].astype(f32) + n_ref[c, :].astype(f32)) for c in at]
            keep_ref[:, k * wide : (k + 1) * wide] = mine
            place = 2 * block + step + k * wide
            out_ref[place : place + wide, :] = split2(other, 0)

    return call(
        body,
        (arr((2 * block + step + half, wide), bf16), arr((wide // 2, half), f32)),
        (own, near_by),
    )


def first_logits(ours, theirs, mixed):
    step, width = ours.shape
    half = mixed.shape[0] // 2

    def body(a_ref, b_ref, m_ref, out_ref):
        weight = jnp.concatenate([a_ref[...], b_ref[...]], axis=0)
        row = 1 - lax.axis_index("tensor") // 2
        tokens = m_ref[pl.ds(pl.multiple_of(row * half, half), half), :]
        logits = lax.dot_general(weight, tokens, NT, preferred_element_type=f32)
        out_ref[...] = logits.astype(bf16)

    return call(
        body, arr((2 * step, half), bf16), (ours, theirs, mixed), 4 * step * half * width
    )


def gather_shares(own, cross, keep, block, step):
    wide = own.shape[1]
    parts = keep.shape[1] // wide
    begin = 2 * block

    def body(o_ref, c_ref, k_ref, out_ref, side_ref):
        me = lax.axis_index("tensor")
        for ref, share in ((o_ref, me), (c_ref, 3 - me)):
            for k, place in enumerate((share, share ^ 1)):
                place = pl.multiple_of(place * block, block)
                out_ref[pl.ds(place, block), :] = ref[k * block : (k + 1) * block, :]
        u = o_ref[begin : begin + step, :].astype(f32) + c_ref[begin : begin + step, :].astype(f32)
        out_ref[4 * block :, :] = split2(u[:, : wide // 2] + u[:, wide // 2 :], 1)
        for k in range(parts):
            cols = slice(k * wide, (k + 1) * wide)
            at = begin + step + k * wide
            side_ref[:, cols] = k_ref[:, cols] + halve(c_ref[at : at + wide, :].astype(f32))

    return call(
        body,
        (arr((4 * block + step, wide), bf16), arr(keep.shape, f32)),
        (own, cross, keep),
        0,
    )


def pass_on(x):
    def body(x_ref, out_ref):
        out_ref[...] = x_ref[...]

    return call(body, arr(x.shape, x.dtype), (x,), 1 << 30)


def stack(pieces):
    high = pieces[0].shape[0]

    def body(*refs):
        for k, ref in enumerate(refs[:-1]):
            refs[-1][k * high : (k + 1) * high, :] = ref[...]

    return call(body, arr((high * len(pieces), pieces[0].shape[1]), bf16), tuple(pieces))


def logit_rows(folded, mixed, *after):
    slots = list(folded)
    step, width = folded[0].shape
    vocab = step * len(folded)
    half = mixed.shape[0] // 2

    def body(*refs):
        parts, refs = refs[: len(folded)], refs[len(folded) :]
        m_ref, (keep_ref, near_ref, other_ref, rest_ref) = refs[0], refs[-4:]
        row = lax.axis_index("tensor") // 2
        weight = jnp.concatenate([parts[slots.index(k)][...] for k in range(len(slots))], axis=0)
        tokens = m_ref[pl.ds(pl.multiple_of((1 - row) * half, half), half), :]
        other = lax.dot_general(weight, tokens, NT, preferred_element_type=f32).astype(bf16)
        other_ref[...] = other
        rest_ref[...] = other[2 * step :]
        tokens = m_ref[pl.ds(pl.multiple_of(row * half, half), half), :]
        mine = lax.dot_general(weight, tokens, NT, preferred_element_type=f32)
        keep_ref[...] = mine
        near_ref[...] = mine.astype(bf16)

    whole = (vocab, half)
    return call(
        body,
        (arr(whole, f32), arr(whole, bf16), arr(whole, bf16), arr((vocab - 2 * step, half), bf16)),
        (*folded.values(), mixed, *after),
        4 * vocab * half * width,
    )


def token_grads(parts, pieces, first, side_in, targets, lengths):
    vocab, length = pieces[0].shape
    rank = side_in.shape[0]
    step = vocab // parts

    def body(k_ref, n_ref, c_ref, f_ref, l_ref, side_ref, t_ref, live_ref, out_ref):
        row = lax.axis_index("tensor") // 2
        own = lax.axis_index("dp") % parts
        total = k_ref[...] + n_ref[...].astype(f32) + c_ref[...].astype(f32)
        total += jnp.concatenate([l_ref[...], f_ref[...]], axis=0).astype(f32)
        expo = jnp.exp(total)
        targets_here = jnp.where(row == 0, t_ref[0:1, :], t_ref[1:2, :])
        lengths_here = jnp.where(row == 0, live_ref[0:1, :], live_ref[1:2, :])
        live = lax.broadcasted_iota(jnp.int32, (1, length), 1) < lengths_here
        scale = jnp.where(live, 1.0 / jnp.sum(expo, axis=0, keepdims=True), 0.0)
        ids = lax.broadcasted_iota(jnp.int32, (vocab, length), 0) ^ (own * step)
        targets_here = jnp.where(live, targets_here, -1)
        grad = (expo * scale - jnp.where(ids == targets_here, 1.0, 0.0)).astype(bf16)
        joint = lax.dot_general(split2(side_ref[...], 0), grad, NT, preferred_element_type=f32)
        out_ref[...] = split2(halve(joint), 0)

    spread = jnp.broadcast_to(lengths[:, None], targets.shape)
    return call(
        body,
        arr((2 * rank, vocab), bf16),
        (*pieces, first, side_in, targets, spread),
        1 << 34,
    )


def row_scores(parts, joint, shares, queries):
    wide, vocab = joint.shape
    rank = wide // 2
    step = vocab // parts
    lines = rank // 2
    count = parts if queries is None else queries.shape[0]
    high = shares[0].shape[0] // 2
    rows = (high - step) // lines
    extra_args = () if queries is None else (queries,)

    def body(j_ref, a_ref, b_ref, c_ref, d_ref, *refs):
        q_ref, refs = (None, refs) if queries is None else (refs[0], refs[1:])
        out_ref, hold = refs
        own = lax.axis_index("dp") % parts
        s_refs = []
        for begin, pair in ((0, (a_ref, b_ref)), (1, (c_ref, d_ref)), (1, (a_ref, b_ref)), (0, (c_ref, d_ref))):
            s_refs += [ref.at[pl.ds(begin * high, high), :] for ref in pair]
        u = jnp.concatenate([ref[rows * lines :, :] for ref in s_refs], axis=0)
        grads = halve(jnp.dot(j_ref[...], u, preferred_element_type=f32))
        grads = grads[:, :rank] + grads[:, rank:]
        grads = jnp.concatenate([grads[:lines], grads[lines:]], axis=1)
        norm = jnp.sum(grads * grads, keepdims=True)
        low = grads.astype(bf16).astype(f32)
        for k in range(count):
            block = s_refs[k][: rows * lines, :] if q_ref is None else q_ref[k]
            terms = block.astype(f32).reshape(lines, rows, wide) * low[:, None, :]
            place = k if q_ref is not None else k ^ own
            at = pl.ds(pl.multiple_of(place * rows, rows), rows)
            hold[at, :] = split2(jnp.sum(terms, axis=0), 1)
        ones = jnp.ones((16, 2 * wide), bf16)
        inner = lax.dot_general(ones, hold[...], NT, preferred_element_type=f32)
        out_ref[...] = inner[:8] / jnp.sqrt(norm + eps)

    return call(
        body,
        arr((8, count * rows), f32),
        (joint, *shares, *extra_args),
        2 * vocab * rank * rank,
        scratch=[pltpu.VMEM((count * rows, 2 * wide), bf16)],
    )


def join_rows(own, crossed):
    def body(o_ref, c_ref, out_ref):
        first = lax.axis_index("tensor") < 2
        out_ref[0:1] = jnp.where(first, o_ref[0:1], c_ref[0:1])
        out_ref[1:2] = jnp.where(first, c_ref[0:1], o_ref[0:1])

    return call(body, arr(own.shape, f32), (own, crossed))


def pick_rows(joined, came):
    def body(j_ref, c_ref, out_ref):
        me = lax.axis_index("tensor")
        out_ref[...] = jnp.where((me == 1) | (me == 2), j_ref[0:2], c_ref[0:2])

    return call(body, arr((2, joined.shape[1]), f32), (joined, came))


def per_device(
    hidden, targets, lengths, conv_filter, proj_weight, unembed, proj_in, proj_out, query_grads
):
    rows = hidden.shape[0]
    n_dp, n_t = lax.axis_size("dp"), lax.axis_size("tensor")
    assert n_t == 4 and rows == 2
    parts = min(n_dp, 8)

    def send(x, pairs):
        return lax.ppermute(x, "tensor", pairs)

    def cross(x):
        pairs = [(d * 4 + a, e * 4 + b) for d in range(n_dp) for a, e, b in (
            (0, d ^ 1, 0), (1, d, 2), (2, d, 1), (3, d ^ 1, 3))]
        return lax.ppermute(x, ("dp", "tensor"), pairs)

    def swap(x, axis, slot):
        return lax.ppermute(x, axis, [(i, i ^ slot) for i in range(lax.axis_size(axis))])

    start = own_rows(parts, unembed)
    came = {s: swap(start, "tensor", s) for s in (2, 3, 1)}
    mixed, shares, folding, weight = local_work(
        hidden, conv_filter, proj_in.T, proj_out.T, query_grads, start, proj_weight
    )
    shares_near = send(shares, NEAR)
    for s in (2, 1, 3):
        folding = fold_more(folding, came[s], weight, s, bf16 if s == 3 else f32)
    block, step, half = query_grads.size // 128, start.shape[0], hidden.shape[1]
    across, keep_side = relay_shares(shares, shares_near, block, step, half)
    folded = {s: swap(folding, "dp", s) for s in reversed(range(2, parts, 2))}
    folded[0] = folding
    folded |= {s + 1: swap(x, "dp", 1) for s, x in folded.items()}
    first = pass_on(send(first_logits(folded[0], folded[1], mixed), FAR))
    whole, side_in = gather_shares(across, cross(across), keep_side, block, step)
    keep, near_logits, other_logits, rest = logit_rows(folded, mixed, side_in, first)
    pieces = (keep, send(near_logits, NEAR), cross(other_logits), send(rest, FAR))
    queries = None
    if n_dp != parts:
        queries = lax.all_gather(whole[: 4 * block], "dp", axis=0)
    others = {s: swap(whole, "dp", s) for s in range(2, parts, 2)}
    pairs = stack((whole, others[4])), stack((others[6], others[2]))
    shares = [y for x in pairs for y in (x, swap(x, "dp", 1))]
    joint = token_grads(parts, pieces, first, side_in, targets, lengths)
    scores = row_scores(parts, joint, shares, queries)
    joined = join_rows(scores, cross(scores))
    return pick_rows(joined, send(joined, NEAR))


def solution(mesh):
    in_specs = (
        P("dp", None, "tensor"),
        P("dp", None),
        P("dp"),
        P(None, "tensor"),
        P("tensor", None),
        P(None, "tensor"),
        P("tensor", None),
        P("tensor", None),
        P("dp", "tensor"),
    )
    return jax.shard_map(
        per_device, mesh=mesh, in_specs=in_specs, out_specs=P("dp", None), check_vma=False
    )
```

```python
import jax
import jax.numpy as jnp
from jax import lax
from jax.experimental import pallas as pl
from jax.experimental.pallas import tpu as pltpu
from jax.sharding import PartitionSpec as P

eps = 1e-06
f32, bf16 = jnp.float32, jnp.bfloat16
NT = (((1,), (1,)), ((), ()))
TN = (((0,), (0,)), ((), ()))
VM = pl.BlockSpec(memory_space=pltpu.VMEM)
ANY = pl.BlockSpec(memory_space=pl.ANY)
NEAR = [(0, 1), (1, 0), (2, 3), (3, 2)]
FAR = [(0, 2), (3, 1), (1, 0), (2, 3)]


def split2(value, axis):
    high = value.astype(bf16)
    low = (value - high.astype(f32)).astype(bf16)
    return jnp.concatenate([high, low], axis=axis)


def arr(shape, dtype):
    return jax.ShapeDtypeStruct(shape, dtype)


def call(body, outs, args, flops=0, in_specs=None, scratch=()):
    moved = sum(a.size * a.dtype.itemsize for a in args)
    return pl.pallas_call(
        body,
        out_shape=outs,
        in_specs=in_specs or [VM] * len(args),
        out_specs=jax.tree.map(lambda _: VM, outs),
        scratch_shapes=list(scratch),
        cost_estimate=pl.CostEstimate(flops=flops, bytes_accessed=moved, transcendentals=0),
        compiler_params=pltpu.CompilerParams(vmem_limit_bytes=32 << 20),
    )(*args)


def near(x):
    return pltpu.with_memory_space_constraint(x, pltpu.VMEM)


def far(x):
    return pltpu.with_memory_space_constraint(x, pltpu.HBM)


def own_rows(parts, unembed):
    vocab, width = unembed.shape
    step = vocab // parts

    def body(e_ref, out_ref, sem):
        own = pl.multiple_of((lax.axis_index("dp") % parts) * step, step)
        copy = pltpu.make_async_copy(e_ref.at[pl.ds(own, step), :], out_ref, sem)
        copy.start()
        copy.wait()

    return call(
        body,
        arr((step, width), bf16),
        (far(unembed),),
        in_specs=[ANY],
        scratch=[pltpu.SemaphoreType.DMA],
    )


def fold_term(rows, w_ref, share):
    width = rows.shape[1]
    cols = pl.ds(pl.multiple_of(share * width, width), width)
    return lax.dot_general(rows, w_ref[:, cols], NT, preferred_element_type=f32)


def local_work(hidden, conv_filter, proj_in_t, proj_out_t, query_grads, start, proj_weight):
    rows, length, width = hidden.shape
    rank = proj_in_t.shape[0]
    step = start.shape[0]
    tokens = rows * length
    wide = 2 * rank
    q_rows = query_grads.shape[0]
    lines = width // wide
    u_begin = lines * q_rows
    side_begin = u_begin + step

    def body(
        h_any, p_any, o_any, w_any, c_ref, q_ref, b_ref,
        mixed_ref, out_ref, fold_ref, w_ref, h_ref, p_ref, o_ref, hold, sems,
    ):
        pairs = ((h_any, h_ref), (p_any, p_ref), (o_any, o_ref), (w_any, w_ref))
        copies = [pltpu.make_async_copy(a, b, sems.at[k]) for k, (a, b) in enumerate(pairs)]
        for copy in copies:
            copy.start()
        taps = c_ref[...].astype(f32)
        place = lax.broadcasted_iota(jnp.int32, (length, width), 0)
        copies[0].wait()
        for row in range(rows):
            here = h_ref[row].astype(f32)
            first = jnp.where(place >= 1, pltpu.roll(here, 1, 0), 0.0)
            second = jnp.where(place >= 2, pltpu.roll(here, 2, 0), 0.0)
            mixed_ref[pl.ds(row * length, length), :] = (
                taps[0:1] * here + taps[1:2] * first + taps[2:3] * second
            ).astype(bf16)
        copies[1].wait()
        side = lax.dot_general(p_ref[...], mixed_ref[...], NT, preferred_element_type=f32)
        for k in range(tokens // wide):
            hold[k] = side[:, k * wide : (k + 1) * wide]
        for k in range(tokens // wide):
            pair = [hold[k, pl.ds(odd, rank // 2, stride=2), :] for odd in (0, 1)]
            begin = side_begin + k * wide
            out_ref[begin : begin + wide, :] = split2(jnp.concatenate(pair, axis=0), 0)
        for k in range(lines):
            out_ref[k * q_rows : (k + 1) * q_rows, :] = q_ref[:, k * wide : (k + 1) * wide]
        copies[2].wait()
        u = lax.dot_general(b_ref[...], o_ref[...], NT, preferred_element_type=f32)
        out_ref[u_begin:side_begin, :] = split2(u, 1)
        copies[3].wait()
        fold_ref[...] = fold_term(b_ref[...], w_ref, lax.axis_index("tensor"))

    return call(
        body,
        (
            arr((tokens, width), bf16),
            arr((side_begin + tokens, wide), bf16),
            arr((step, width), f32),
            pltpu.VMEM(proj_weight.shape, bf16),
        ),
        (far(hidden), far(proj_in_t), far(proj_out_t), far(proj_weight), conv_filter, query_grads, start),
        2 * tokens * width * rank + 2 * step * width * width,
        in_specs=[ANY] * 4 + [VM] * 3,
        scratch=[
            pltpu.VMEM(hidden.shape, bf16),
            pltpu.VMEM(proj_in_t.shape, bf16),
            pltpu.VMEM(proj_out_t.shape, bf16),
            pltpu.VMEM((tokens // wide, rank, wide), f32),
            pltpu.SemaphoreType.DMA((4,)),
        ],
    )


def fold_more(so_far, block, weight, slot, dtype):
    step, width = block.shape

    def body(f_ref, b_ref, w_ref, out_ref):
        share = lax.axis_index("tensor") ^ slot
        out_ref[...] = (f_ref[...] + fold_term(b_ref[...], w_ref, share)).astype(dtype)

    return call(
        body, arr((step, width), dtype), (so_far, block, near(weight)), 2 * step * width * width
    )


def halve(value):
    half = value.shape[0] // 2
    return value[:half] + value[half:]


def relay_shares(own, near_by, block, step, half):
    wide = own.shape[1]
    begin = block + step
    parts = half // wide

    def body(o_ref, n_ref, out_ref, keep_ref):
        row = lax.axis_index("tensor") // 2
        out_ref[:block, :] = o_ref[:block, :]
        out_ref[block : 2 * block, :] = n_ref[:block, :]
        u = o_ref[block:begin, :].astype(f32) + n_ref[block:begin, :].astype(f32)
        out_ref[2 * block : 2 * block + step, :] = split2(u[:, : wide // 2] + u[:, wide // 2 :], 1)
        for k in range(parts):
            at = [pl.ds(pl.multiple_of(begin + (r * parts + k) * wide, wide // 2), wide) for r in (row, 1 - row)]
            mine, other = [halve(o_ref[c, :].astype(f32) + n_ref[c, :].astype(f32)) for c in at]
            keep_ref[:, k * wide : (k + 1) * wide] = mine
            place = 2 * block + step + k * wide
            out_ref[place : place + wide, :] = split2(other, 0)

    return call(
        body,
        (arr((2 * block + step + half, wide), bf16), arr((wide // 2, half), f32)),
        (own, near_by),
    )


def first_logits(ours, theirs, mixed):
    step, width = ours.shape
    half = mixed.shape[0] // 2

    def body(a_ref, b_ref, m_ref, out_ref):
        weight = jnp.concatenate([a_ref[...], b_ref[...]], axis=0)
        row = 1 - lax.axis_index("tensor") // 2
        tokens = m_ref[pl.ds(pl.multiple_of(row * half, half), half), :]
        logits = lax.dot_general(weight, tokens, NT, preferred_element_type=f32)
        out_ref[...] = logits.astype(bf16)

    return call(
        body, arr((2 * step, half), bf16), (ours, theirs, mixed), 4 * step * half * width
    )


def gather_shares(own, cross, keep, block, step):
    wide = own.shape[1]
    parts = keep.shape[1] // wide
    begin = 2 * block

    def body(o_ref, c_ref, k_ref, out_ref, side_ref):
        me = lax.axis_index("tensor")
        for ref, share in ((o_ref, me), (c_ref, 3 - me)):
            for k, place in enumerate((share, share ^ 1)):
                place = pl.multiple_of(place * block, block)
                out_ref[pl.ds(place, block), :] = ref[k * block : (k + 1) * block, :]
        u = o_ref[begin : begin + step, :].astype(f32) + c_ref[begin : begin + step, :].astype(f32)
        out_ref[4 * block :, :] = split2(u[:, : wide // 2] + u[:, wide // 2 :], 1)
        for k in range(parts):
            cols = slice(k * wide, (k + 1) * wide)
            at = begin + step + k * wide
            side_ref[:, cols] = k_ref[:, cols] + halve(c_ref[at : at + wide, :].astype(f32))

    return call(
        body,
        (arr((4 * block + step, wide), bf16), arr(keep.shape, f32)),
        (own, cross, keep),
        0,
    )


def pass_on(x):
    def body(x_ref, out_ref):
        out_ref[...] = x_ref[...]

    return call(body, arr(x.shape, x.dtype), (x,), 1 << 30)


def stack(pieces):
    high = pieces[0].shape[0]

    def body(*refs):
        for k, ref in enumerate(refs[:-1]):
            refs[-1][k * high : (k + 1) * high, :] = ref[...]

    return call(body, arr((high * len(pieces), pieces[0].shape[1]), bf16), tuple(pieces))


def logit_rows(folded, mixed, *after):
    slots = list(folded)
    step, width = folded[0].shape
    vocab = step * len(folded)
    half = mixed.shape[0] // 2

    def body(*refs):
        parts, refs = refs[: len(folded)], refs[len(folded) :]
        m_ref, (keep_ref, near_ref, other_ref, rest_ref) = refs[0], refs[-4:]
        row = lax.axis_index("tensor") // 2
        weight = jnp.concatenate([parts[slots.index(k)][...] for k in range(len(slots))], axis=0)
        tokens = m_ref[pl.ds(pl.multiple_of((1 - row) * half, half), half), :]
        other = lax.dot_general(weight, tokens, NT, preferred_element_type=f32).astype(bf16)
        other_ref[...] = other
        rest_ref[...] = other[2 * step :]
        tokens = m_ref[pl.ds(pl.multiple_of(row * half, half), half), :]
        mine = lax.dot_general(weight, tokens, NT, preferred_element_type=f32)
        keep_ref[...] = mine
        near_ref[...] = mine.astype(bf16)

    whole = (vocab, half)
    return call(
        body,
        (arr(whole, f32), arr(whole, bf16), arr(whole, bf16), arr((vocab - 2 * step, half), bf16)),
        (*folded.values(), mixed, *after),
        4 * vocab * half * width,
    )


def join(first, rest):
    high = first.shape[0]
    shape = (high + rest.shape[0], first.shape[1])

    def body(a_ref, b_ref, out_ref):
        out_ref[:high, :] = a_ref[...]
        out_ref[high:, :] = b_ref[...]

    return call(body, arr(shape, bf16), (first, rest), 1 << 30)


def token_grads(parts, pieces, side_in, targets, lengths):
    vocab, length = pieces[0].shape
    rank = side_in.shape[0]
    step = vocab // parts

    def body(k_ref, f_ref, c_ref, n_ref, side_ref, t_ref, live_ref, out_ref):
        row = lax.axis_index("tensor") // 2
        own = lax.axis_index("dp") % parts
        total = k_ref[...]
        for ref in (f_ref, c_ref, n_ref):
            total += ref[...].astype(f32)
        expo = jnp.exp(total)
        targets_here = jnp.where(row == 0, t_ref[0:1, :], t_ref[1:2, :])
        lengths_here = jnp.where(row == 0, live_ref[0:1, :], live_ref[1:2, :])
        live = lax.broadcasted_iota(jnp.int32, (1, length), 1) < lengths_here
        scale = jnp.where(live, 1.0 / jnp.sum(expo, axis=0, keepdims=True), 0.0)
        ids = lax.broadcasted_iota(jnp.int32, (vocab, length), 0) ^ (own * step)
        targets_here = jnp.where(live, targets_here, -1)
        grad = (expo * scale - jnp.where(ids == targets_here, 1.0, 0.0)).astype(bf16)
        joint = lax.dot_general(split2(side_ref[...], 0), grad, NT, preferred_element_type=f32)
        out_ref[...] = split2(halve(joint), 0)

    spread = jnp.broadcast_to(lengths[:, None], targets.shape)
    return call(
        body,
        arr((2 * rank, vocab), bf16),
        (*pieces, side_in, targets, spread),
        1 << 34,
    )


def row_scores(parts, joint, shares, queries):
    wide, vocab = joint.shape
    rank = wide // 2
    step = vocab // parts
    lines = rank // 2
    count = parts if queries is None else queries.shape[0]
    high = shares[0].shape[0] // 2
    rows = (high - step) // lines
    extra_args = () if queries is None else (queries,)

    def body(j_ref, a_ref, b_ref, c_ref, d_ref, *refs):
        q_ref, refs = (None, refs) if queries is None else (refs[0], refs[1:])
        out_ref, hold = refs
        own = lax.axis_index("dp") % parts
        s_refs = []
        for begin, pair in ((0, (a_ref, b_ref)), (1, (c_ref, d_ref)), (1, (a_ref, b_ref)), (0, (c_ref, d_ref))):
            s_refs += [ref.at[pl.ds(begin * high, high), :] for ref in pair]
        u = jnp.concatenate([ref[rows * lines :, :] for ref in s_refs], axis=0)
        grads = halve(jnp.dot(j_ref[...], u, preferred_element_type=f32))
        grads = grads[:, :rank] + grads[:, rank:]
        grads = jnp.concatenate([grads[:lines], grads[lines:]], axis=1)
        norm = jnp.sum(grads * grads, keepdims=True)
        low = grads.astype(bf16).astype(f32)
        for k in range(count):
            block = s_refs[k][: rows * lines, :] if q_ref is None else q_ref[k]
            terms = block.astype(f32).reshape(lines, rows, wide) * low[:, None, :]
            place = k if q_ref is not None else k ^ own
            at = pl.ds(pl.multiple_of(place * rows, rows), rows)
            hold[at, :] = split2(jnp.sum(terms, axis=0), 1)
        ones = jnp.ones((16, 2 * wide), bf16)
        inner = lax.dot_general(ones, hold[...], NT, preferred_element_type=f32)
        out_ref[...] = inner[:8] / jnp.sqrt(norm + eps)

    return call(
        body,
        arr((8, count * rows), f32),
        (joint, *shares, *extra_args),
        2 * vocab * rank * rank,
        scratch=[pltpu.VMEM((count * rows, 2 * wide), bf16)],
    )


def join_rows(own, crossed):
    def body(o_ref, c_ref, out_ref):
        first = lax.axis_index("tensor") < 2
        out_ref[0:1] = jnp.where(first, o_ref[0:1], c_ref[0:1])
        out_ref[1:2] = jnp.where(first, c_ref[0:1], o_ref[0:1])

    return call(body, arr(own.shape, f32), (own, crossed))


def pick_rows(joined, came):
    def body(j_ref, c_ref, out_ref):
        me = lax.axis_index("tensor")
        out_ref[...] = jnp.where((me == 1) | (me == 2), j_ref[0:2], c_ref[0:2])

    return call(body, arr((2, joined.shape[1]), f32), (joined, came))


def per_device(
    hidden, targets, lengths, conv_filter, proj_weight, unembed, proj_in, proj_out, query_grads
):
    rows = hidden.shape[0]
    n_dp, n_t = lax.axis_size("dp"), lax.axis_size("tensor")
    assert n_t == 4 and rows == 2
    parts = min(n_dp, 8)

    def send(x, pairs):
        return lax.ppermute(x, "tensor", pairs)

    def cross(x):
        pairs = [(d * 4 + a, e * 4 + b) for d in range(n_dp) for a, e, b in (
            (0, d ^ 1, 0), (1, d, 2), (2, d, 1), (3, d ^ 1, 3))]
        return lax.ppermute(x, ("dp", "tensor"), pairs)

    def swap(x, axis, slot):
        return lax.ppermute(x, axis, [(i, i ^ slot) for i in range(lax.axis_size(axis))])

    start = own_rows(parts, unembed)
    came = {s: swap(start, "tensor", s) for s in (2, 3, 1)}
    mixed, shares, folding, weight = local_work(
        hidden, conv_filter, proj_in.T, proj_out.T, query_grads, start, proj_weight
    )
    shares_near = send(shares, NEAR)
    for s in (2, 1, 3):
        folding = fold_more(folding, came[s], weight, s, bf16 if s == 3 else f32)
    block, step, half = query_grads.size // 128, start.shape[0], hidden.shape[1]
    across, keep_side = relay_shares(shares, shares_near, block, step, half)
    folded = {s: swap(folding, "dp", s) for s in reversed(range(2, parts, 2))}
    folded[0] = folding
    folded |= {s + 1: swap(x, "dp", 1) for s, x in folded.items()}
    first = pass_on(send(first_logits(folded[0], folded[1], mixed), FAR))
    whole, side_in = gather_shares(across, cross(across), keep_side, block, step)
    keep, near_logits, other_logits, rest = logit_rows(folded, mixed, side_in, first)
    far_logits = join(first, send(rest, FAR))
    pieces = (keep, far_logits, cross(other_logits), send(near_logits, NEAR))
    queries = None
    if n_dp != parts:
        queries = lax.all_gather(whole[: 4 * block], "dp", axis=0)
    others = {s: swap(whole, "dp", s) for s in range(2, parts, 2)}
    pairs = stack((whole, others[4])), stack((others[6], others[2]))
    shares = [y for x in pairs for y in (x, swap(x, "dp", 1))]
    joint = token_grads(parts, pieces, side_in, targets, lengths)
    scores = row_scores(parts, joint, shares, queries)
    joined = join_rows(scores, cross(scores))
    return pick_rows(joined, send(joined, NEAR))


def solution(mesh):
    in_specs = (
        P("dp", None, "tensor"),
        P("dp", None),
        P("dp"),
        P(None, "tensor"),
        P("tensor", None),
        P(None, "tensor"),
        P("tensor", None),
        P("tensor", None),
        P("dp", "tensor"),
    )
    return jax.shard_map(
        per_device, mesh=mesh, in_specs=in_specs, out_specs=P("dp", None), check_vma=False
    )
```

```python
import jax
import jax.numpy as jnp
from jax import lax
from jax.experimental import pallas as pl
from jax.experimental.pallas import tpu as pltpu
from jax.sharding import PartitionSpec as P

eps = 1e-06
f32, bf16 = jnp.float32, jnp.bfloat16
NT = (((1,), (1,)), ((), ()))
TN = (((0,), (0,)), ((), ()))
VM = pl.BlockSpec(memory_space=pltpu.VMEM)
ANY = pl.BlockSpec(memory_space=pl.ANY)
NEAR = [(0, 1), (1, 0), (2, 3), (3, 2)]
FAR = [(0, 2), (3, 1), (1, 0), (2, 3)]


def split2(value, axis):
    high = value.astype(bf16)
    low = (value - high.astype(f32)).astype(bf16)
    return jnp.concatenate([high, low], axis=axis)


def arr(shape, dtype):
    return jax.ShapeDtypeStruct(shape, dtype)


def call(body, outs, args, flops=0, in_specs=None, scratch=()):
    moved = sum(a.size * a.dtype.itemsize for a in args)
    return pl.pallas_call(
        body,
        out_shape=outs,
        in_specs=in_specs or [VM] * len(args),
        out_specs=jax.tree.map(lambda _: VM, outs),
        scratch_shapes=list(scratch),
        cost_estimate=pl.CostEstimate(flops=flops, bytes_accessed=moved, transcendentals=0),
        compiler_params=pltpu.CompilerParams(vmem_limit_bytes=32 << 20),
    )(*args)


def near(x):
    return pltpu.with_memory_space_constraint(x, pltpu.VMEM)


def far(x):
    return pltpu.with_memory_space_constraint(x, pltpu.HBM)


def own_rows(parts, unembed):
    vocab, width = unembed.shape
    step = vocab // parts

    def body(e_ref, out_ref, sem):
        own = pl.multiple_of((lax.axis_index("dp") % parts) * step, step)
        copy = pltpu.make_async_copy(e_ref.at[pl.ds(own, step), :], out_ref, sem)
        copy.start()
        copy.wait()

    return call(
        body,
        arr((step, width), bf16),
        (far(unembed),),
        in_specs=[ANY],
        scratch=[pltpu.SemaphoreType.DMA],
    )


def fold_term(rows, w_ref, share):
    width = rows.shape[1]
    cols = pl.ds(pl.multiple_of(share * width, width), width)
    return lax.dot_general(rows, w_ref[:, cols], NT, preferred_element_type=f32)


def local_work(hidden, conv_filter, proj_in_t, proj_out_t, query_grads, start, proj_weight):
    rows, length, width = hidden.shape
    rank = proj_in_t.shape[0]
    step = start.shape[0]
    tokens = rows * length
    wide = 2 * rank
    q_rows = query_grads.shape[0]
    lines = width // wide
    u_begin = lines * q_rows
    side_begin = u_begin + step

    def body(
        h_any, p_any, o_any, w_any, c_ref, q_ref, b_ref,
        mixed_ref, out_ref, fold_ref, w_ref, h_ref, p_ref, o_ref, hold, sems,
    ):
        pairs = ((h_any, h_ref), (p_any, p_ref), (o_any, o_ref), (w_any, w_ref))
        copies = [pltpu.make_async_copy(a, b, sems.at[k]) for k, (a, b) in enumerate(pairs)]
        for copy in copies:
            copy.start()
        taps = c_ref[...].astype(f32)
        place = lax.broadcasted_iota(jnp.int32, (length, width), 0)
        copies[0].wait()
        for row in range(rows):
            here = h_ref[row].astype(f32)
            first = jnp.where(place >= 1, pltpu.roll(here, 1, 0), 0.0)
            second = jnp.where(place >= 2, pltpu.roll(here, 2, 0), 0.0)
            mixed_ref[pl.ds(row * length, length), :] = (
                taps[0:1] * here + taps[1:2] * first + taps[2:3] * second
            ).astype(bf16)
        copies[1].wait()
        side = lax.dot_general(p_ref[...], mixed_ref[...], NT, preferred_element_type=f32)
        for k in range(tokens // wide):
            hold[k] = side[:, k * wide : (k + 1) * wide]
        for k in range(tokens // wide):
            pair = [hold[k, pl.ds(odd, rank // 2, stride=2), :] for odd in (0, 1)]
            begin = side_begin + k * rank
            out_ref[begin : begin + rank, :] = jnp.concatenate(pair, axis=0).astype(bf16)
        for k in range(lines):
            out_ref[k * q_rows : (k + 1) * q_rows, :] = q_ref[:, k * wide : (k + 1) * wide]
        copies[2].wait()
        u = lax.dot_general(b_ref[...], o_ref[...], NT, preferred_element_type=f32)
        out_ref[u_begin:side_begin, :] = split2(u, 1)
        copies[3].wait()
        fold_ref[...] = fold_term(b_ref[...], w_ref, lax.axis_index("tensor"))

    return call(
        body,
        (
            arr((tokens, width), bf16),
            arr((side_begin + tokens // wide * rank, wide), bf16),
            arr((step, width), f32),
            pltpu.VMEM(proj_weight.shape, bf16),
        ),
        (far(hidden), far(proj_in_t), far(proj_out_t), far(proj_weight), conv_filter, query_grads, start),
        2 * tokens * width * rank + 2 * step * width * width,
        in_specs=[ANY] * 4 + [VM] * 3,
        scratch=[
            pltpu.VMEM(hidden.shape, bf16),
            pltpu.VMEM(proj_in_t.shape, bf16),
            pltpu.VMEM(proj_out_t.shape, bf16),
            pltpu.VMEM((tokens // wide, rank, wide), f32),
            pltpu.SemaphoreType.DMA((4,)),
        ],
    )


def fold_more(so_far, block, weight, slot, dtype):
    step, width = block.shape

    def body(f_ref, b_ref, w_ref, out_ref):
        share = lax.axis_index("tensor") ^ slot
        out_ref[...] = (f_ref[...] + fold_term(b_ref[...], w_ref, share)).astype(dtype)

    return call(
        body, arr((step, width), dtype), (so_far, block, near(weight)), 2 * step * width * width
    )


def halve(value):
    half = value.shape[0] // 2
    return value[:half] + value[half:]


def relay_shares(own, near_by, block, step, half):
    wide = own.shape[1]
    begin = block + step
    rank = wide // 2
    parts = half // wide

    def body(o_ref, n_ref, out_ref, keep_ref):
        row = lax.axis_index("tensor") // 2
        out_ref[:block, :] = o_ref[:block, :]
        out_ref[block : 2 * block, :] = n_ref[:block, :]
        u = o_ref[block:begin, :].astype(f32) + n_ref[block:begin, :].astype(f32)
        out_ref[2 * block : 2 * block + step, :] = split2(u[:, : wide // 2] + u[:, wide // 2 :], 1)
        for k in range(parts):
            mine, other = [
                o_ref[at, :].astype(f32) + n_ref[at, :].astype(f32)
                for at in [
                    pl.ds(pl.multiple_of(begin + (r * parts + k) * rank, rank), rank)
                    for r in (row, 1 - row)
                ]
            ]
            keep_ref[:, k * wide : (k + 1) * wide] = mine
            place = 2 * block + step + k * rank
            out_ref[place : place + rank, :] = other.astype(bf16)

    return call(
        body,
        (arr((2 * block + step + parts * rank, wide), bf16), arr((rank, half), f32)),
        (own, near_by),
    )


def first_logits(ours, theirs, mixed):
    step, width = ours.shape
    half = mixed.shape[0] // 2

    def body(a_ref, b_ref, m_ref, out_ref):
        weight = jnp.concatenate([a_ref[...], b_ref[...]], axis=0)
        row = 1 - lax.axis_index("tensor") // 2
        tokens = m_ref[pl.ds(pl.multiple_of(row * half, half), half), :]
        logits = lax.dot_general(weight, tokens, NT, preferred_element_type=f32)
        out_ref[...] = logits.astype(bf16)

    return call(
        body, arr((2 * step, half), bf16), (ours, theirs, mixed), 4 * step * half * width
    )


def gather_shares(own, cross, keep, block, step):
    wide = own.shape[1]
    parts = keep.shape[1] // wide
    begin = 2 * block

    def body(o_ref, c_ref, k_ref, out_ref, side_ref):
        me = lax.axis_index("tensor")
        for ref, share in ((o_ref, me), (c_ref, 3 - me)):
            for k, place in enumerate((share, share ^ 1)):
                place = pl.multiple_of(place * block, block)
                out_ref[pl.ds(place, block), :] = ref[k * block : (k + 1) * block, :]
        u = o_ref[begin : begin + step, :].astype(f32) + c_ref[begin : begin + step, :].astype(f32)
        out_ref[4 * block :, :] = split2(u[:, : wide // 2] + u[:, wide // 2 :], 1)
        for k in range(parts):
            cols = slice(k * wide, (k + 1) * wide)
            at = begin + step + k * (wide // 2)
            side_ref[:, cols] = k_ref[:, cols] + c_ref[at : at + wide // 2, :].astype(f32)

    return call(
        body,
        (arr((4 * block + step, wide), bf16), arr(keep.shape, f32)),
        (own, cross, keep),
        0,
    )


def pass_on(x):
    def body(x_ref, out_ref):
        out_ref[...] = x_ref[...]

    return call(body, arr(x.shape, x.dtype), (x,), 1 << 30)


def stack(pieces):
    high = pieces[0].shape[0]

    def body(*refs):
        for k, ref in enumerate(refs[:-1]):
            refs[-1][k * high : (k + 1) * high, :] = ref[...]

    return call(body, arr((high * len(pieces), pieces[0].shape[1]), bf16), tuple(pieces))


def logit_rows(folded, mixed, *after):
    slots = list(folded)
    step, width = folded[0].shape
    vocab = step * len(folded)
    half = mixed.shape[0] // 2

    def body(*refs):
        parts, refs = refs[: len(folded)], refs[len(folded) :]
        m_ref, (keep_ref, near_ref, other_ref, rest_ref) = refs[0], refs[-4:]
        row = lax.axis_index("tensor") // 2
        weight = jnp.concatenate([parts[slots.index(k)][...] for k in range(len(slots))], axis=0)
        tokens = m_ref[pl.ds(pl.multiple_of((1 - row) * half, half), half), :]
        other = lax.dot_general(weight, tokens, NT, preferred_element_type=f32).astype(bf16)
        other_ref[...] = other
        rest_ref[...] = other[2 * step :]
        tokens = m_ref[pl.ds(pl.multiple_of(row * half, half), half), :]
        mine = lax.dot_general(weight, tokens, NT, preferred_element_type=f32)
        keep_ref[...] = mine
        near_ref[...] = mine.astype(bf16)

    whole = (vocab, half)
    return call(
        body,
        (arr(whole, f32), arr(whole, bf16), arr(whole, bf16), arr((vocab - 2 * step, half), bf16)),
        (*folded.values(), mixed, *after),
        4 * vocab * half * width,
    )


def token_grads(parts, pieces, first, side_in, targets, lengths):
    vocab, length = pieces[0].shape
    rank = side_in.shape[0]
    step = vocab // parts

    def body(k_ref, n_ref, c_ref, f_ref, l_ref, side_ref, t_ref, live_ref, out_ref):
        row = lax.axis_index("tensor") // 2
        own = lax.axis_index("dp") % parts
        total = k_ref[...] + n_ref[...].astype(f32) + c_ref[...].astype(f32)
        total += jnp.concatenate([l_ref[...], f_ref[...]], axis=0).astype(f32)
        expo = jnp.exp(total)
        targets_here = jnp.where(row == 0, t_ref[0:1, :], t_ref[1:2, :])
        lengths_here = jnp.where(row == 0, live_ref[0:1, :], live_ref[1:2, :])
        live = lax.broadcasted_iota(jnp.int32, (1, length), 1) < lengths_here
        scale = jnp.where(live, 1.0 / jnp.sum(expo, axis=0, keepdims=True), 0.0)
        ids = lax.broadcasted_iota(jnp.int32, (vocab, length), 0) ^ (own * step)
        targets_here = jnp.where(live, targets_here, -1)
        grad = (expo * scale - jnp.where(ids == targets_here, 1.0, 0.0)).astype(bf16)
        joint = lax.dot_general(split2(side_ref[...], 0), grad, NT, preferred_element_type=f32)
        out_ref[...] = split2(halve(joint), 0)

    spread = jnp.broadcast_to(lengths[:, None], targets.shape)
    return call(
        body,
        arr((2 * rank, vocab), bf16),
        (*pieces, first, side_in, targets, spread),
        1 << 34,
    )


def row_scores(parts, joint, shares, queries):
    wide, vocab = joint.shape
    rank = wide // 2
    step = vocab // parts
    lines = rank // 2
    count = parts if queries is None else queries.shape[0]
    high = shares[0].shape[0] // 2
    rows = (high - step) // lines
    extra_args = () if queries is None else (queries,)

    def body(j_ref, a_ref, b_ref, c_ref, d_ref, *refs):
        q_ref, refs = (None, refs) if queries is None else (refs[0], refs[1:])
        out_ref, hold = refs
        own = lax.axis_index("dp") % parts
        s_refs = []
        for begin, pair in ((0, (a_ref, b_ref)), (1, (c_ref, d_ref)), (1, (a_ref, b_ref)), (0, (c_ref, d_ref))):
            s_refs += [ref.at[pl.ds(begin * high, high), :] for ref in pair]
        u = jnp.concatenate([ref[rows * lines :, :] for ref in s_refs], axis=0)
        grads = halve(jnp.dot(j_ref[...], u, preferred_element_type=f32))
        grads = grads[:, :rank] + grads[:, rank:]
        grads = jnp.concatenate([grads[:lines], grads[lines:]], axis=1)
        norm = jnp.sum(grads * grads, keepdims=True)
        low = grads.astype(bf16).astype(f32)
        for k in range(count):
            block = s_refs[k][: rows * lines, :] if q_ref is None else q_ref[k]
            terms = block.astype(f32).reshape(lines, rows, wide) * low[:, None, :]
            place = k if q_ref is not None else k ^ own
            at = pl.ds(pl.multiple_of(place * rows, rows), rows)
            hold[at, :] = split2(jnp.sum(terms, axis=0), 1)
        ones = jnp.ones((16, 2 * wide), bf16)
        inner = lax.dot_general(ones, hold[...], NT, preferred_element_type=f32)
        out_ref[...] = inner[:8] / jnp.sqrt(norm + eps)

    return call(
        body,
        arr((8, count * rows), f32),
        (joint, *shares, *extra_args),
        2 * vocab * rank * rank,
        scratch=[pltpu.VMEM((count * rows, 2 * wide), bf16)],
    )


def join_rows(own, crossed):
    def body(o_ref, c_ref, out_ref):
        first = lax.axis_index("tensor") < 2
        out_ref[0:1] = jnp.where(first, o_ref[0:1], c_ref[0:1])
        out_ref[1:2] = jnp.where(first, c_ref[0:1], o_ref[0:1])

    return call(body, arr(own.shape, f32), (own, crossed))


def pick_rows(joined, came):
    def body(j_ref, c_ref, out_ref):
        me = lax.axis_index("tensor")
        out_ref[...] = jnp.where((me == 1) | (me == 2), j_ref[0:2], c_ref[0:2])

    return call(body, arr((2, joined.shape[1]), f32), (joined, came))


def per_device(
    hidden, targets, lengths, conv_filter, proj_weight, unembed, proj_in, proj_out, query_grads
):
    rows = hidden.shape[0]
    n_dp, n_t = lax.axis_size("dp"), lax.axis_size("tensor")
    assert n_t == 4 and rows == 2
    parts = min(n_dp, 8)

    def send(x, pairs):
        return lax.ppermute(x, "tensor", pairs)

    def cross(x):
        pairs = [(d * 4 + a, e * 4 + b) for d in range(n_dp) for a, e, b in (
            (0, d ^ 1, 0), (1, d, 2), (2, d, 1), (3, d ^ 1, 3))]
        return lax.ppermute(x, ("dp", "tensor"), pairs)

    def swap(x, axis, slot):
        return lax.ppermute(x, axis, [(i, i ^ slot) for i in range(lax.axis_size(axis))])

    start = own_rows(parts, unembed)
    came = {s: swap(start, "tensor", s) for s in (2, 3, 1)}
    mixed, shares, folding, weight = local_work(
        hidden, conv_filter, proj_in.T, proj_out.T, query_grads, start, proj_weight
    )
    shares_near = send(shares, NEAR)
    for s in (2, 1, 3):
        folding = fold_more(folding, came[s], weight, s, bf16 if s == 3 else f32)
    block, step, half = query_grads.size // 128, start.shape[0], hidden.shape[1]
    across, keep_side = relay_shares(shares, shares_near, block, step, half)
    folded = {s: swap(folding, "dp", s) for s in reversed(range(2, parts, 2))}
    folded[0] = folding
    folded |= {s + 1: swap(x, "dp", 1) for s, x in folded.items()}
    first = pass_on(send(first_logits(folded[0], folded[1], mixed), FAR))
    whole, side_in = gather_shares(across, cross(across), keep_side, block, step)
    keep, near_logits, other_logits, rest = logit_rows(folded, mixed, side_in, first)
    pieces = (keep, send(near_logits, NEAR), cross(other_logits), send(rest, FAR))
    queries = None
    if n_dp != parts:
        queries = lax.all_gather(whole[: 4 * block], "dp", axis=0)
    others = {s: swap(whole, "dp", s) for s in range(2, parts, 2)}
    pairs = stack((whole, others[4])), stack((others[6], others[2]))
    shares = [y for x in pairs for y in (x, swap(x, "dp", 1))]
    joint = token_grads(parts, pieces, first, side_in, targets, lengths)
    scores = row_scores(parts, joint, shares, queries)
    joined = join_rows(scores, cross(scores))
    return pick_rows(joined, send(joined, NEAR))


def solution(mesh):
    in_specs = (
        P("dp", None, "tensor"),
        P("dp", None),
        P("dp"),
        P(None, "tensor"),
        P("tensor", None),
        P(None, "tensor"),
        P("tensor", None),
        P("tensor", None),
        P("dp", "tensor"),
    )
    return jax.shard_map(
        per_device, mesh=mesh, in_specs=in_specs, out_specs=P("dp", None), check_vma=False
    )
```

```python
import jax
import jax.numpy as jnp
from jax import lax
from jax.experimental import pallas as pl
from jax.experimental.pallas import tpu as pltpu
from jax.sharding import PartitionSpec as P

eps = 1e-06
f32, bf16 = jnp.float32, jnp.bfloat16
NT = (((1,), (1,)), ((), ()))
TN = (((0,), (0,)), ((), ()))
VM = pl.BlockSpec(memory_space=pltpu.VMEM)
ANY = pl.BlockSpec(memory_space=pl.ANY)
NEAR = [(0, 1), (1, 0), (2, 3), (3, 2)]
FAR = [(0, 2), (3, 1), (1, 0), (2, 3)]


def split2(value, axis):
    high = value.astype(bf16)
    low = (value - high.astype(f32)).astype(bf16)
    return jnp.concatenate([high, low], axis=axis)


def arr(shape, dtype):
    return jax.ShapeDtypeStruct(shape, dtype)


def call(body, outs, args, flops=0, in_specs=None, scratch=()):
    moved = sum(a.size * a.dtype.itemsize for a in args)
    return pl.pallas_call(
        body,
        out_shape=outs,
        in_specs=in_specs or [VM] * len(args),
        out_specs=jax.tree.map(lambda _: VM, outs),
        scratch_shapes=list(scratch),
        cost_estimate=pl.CostEstimate(flops=flops, bytes_accessed=moved, transcendentals=0),
        compiler_params=pltpu.CompilerParams(vmem_limit_bytes=32 << 20),
    )(*args)


def near(x):
    return pltpu.with_memory_space_constraint(x, pltpu.VMEM)


def far(x):
    return pltpu.with_memory_space_constraint(x, pltpu.HBM)


def own_rows(parts, unembed):
    vocab, width = unembed.shape
    step = vocab // parts

    def body(e_ref, out_ref, sem):
        own = pl.multiple_of((lax.axis_index("dp") % parts) * step, step)
        copy = pltpu.make_async_copy(e_ref.at[pl.ds(own, step), :], out_ref, sem)
        copy.start()
        copy.wait()

    return call(
        body,
        arr((step, width), bf16),
        (far(unembed),),
        in_specs=[ANY],
        scratch=[pltpu.SemaphoreType.DMA],
    )


def fold_term(rows, w_ref, share):
    width = rows.shape[1]
    cols = pl.ds(pl.multiple_of(share * width, width), width)
    return lax.dot_general(rows, w_ref[:, cols], NT, preferred_element_type=f32)


def local_work(hidden, conv_filter, proj_in_t, proj_out_t, query_grads, start, proj_weight):
    rows, length, width = hidden.shape
    rank = proj_in_t.shape[0]
    step = start.shape[0]
    tokens = rows * length
    wide = 2 * rank
    q_rows = query_grads.shape[0]
    lines = width // wide
    u_begin = lines * q_rows
    side_begin = u_begin + step

    def body(
        h_any, p_any, o_any, w_any, c_ref, q_ref, b_ref,
        mixed_ref, out_ref, fold_ref, w_ref, h_ref, p_ref, o_ref, hold, sems,
    ):
        pairs = ((h_any, h_ref), (p_any, p_ref), (o_any, o_ref), (w_any, w_ref))
        copies = [pltpu.make_async_copy(a, b, sems.at[k]) for k, (a, b) in enumerate(pairs)]
        for copy in copies:
            copy.start()
        taps = c_ref[...].astype(f32)
        place = lax.broadcasted_iota(jnp.int32, (length, width), 0)
        copies[0].wait()
        for row in range(rows):
            here = h_ref[row].astype(f32)
            first = jnp.where(place >= 1, pltpu.roll(here, 1, 0), 0.0)
            second = jnp.where(place >= 2, pltpu.roll(here, 2, 0), 0.0)
            mixed_ref[pl.ds(row * length, length), :] = (
                taps[0:1] * here + taps[1:2] * first + taps[2:3] * second
            ).astype(bf16)
        copies[1].wait()
        side = lax.dot_general(p_ref[...], mixed_ref[...], NT, preferred_element_type=f32)
        for k in range(tokens // wide):
            hold[k] = side[:, k * wide : (k + 1) * wide]
        for k in range(tokens // wide):
            pair = [hold[k, pl.ds(odd, rank // 2, stride=2), :] for odd in (0, 1)]
            begin = side_begin + k * rank
            out_ref[begin : begin + rank, :] = jnp.concatenate(pair, axis=0).astype(bf16)
        for k in range(lines):
            out_ref[k * q_rows : (k + 1) * q_rows, :] = q_ref[:, k * wide : (k + 1) * wide]
        copies[2].wait()
        u = lax.dot_general(b_ref[...], o_ref[...], NT, preferred_element_type=f32)
        out_ref[u_begin:side_begin, :] = split2(u, 1)
        copies[3].wait()
        fold_ref[...] = fold_term(b_ref[...], w_ref, lax.axis_index("tensor"))

    return call(
        body,
        (
            arr((tokens, width), bf16),
            arr((side_begin + tokens // wide * rank, wide), bf16),
            arr((step, width), f32),
            pltpu.VMEM(proj_weight.shape, bf16),
        ),
        (far(hidden), far(proj_in_t), far(proj_out_t), far(proj_weight), conv_filter, query_grads, start),
        2 * tokens * width * rank + 2 * step * width * width,
        in_specs=[ANY] * 4 + [VM] * 3,
        scratch=[
            pltpu.VMEM(hidden.shape, bf16),
            pltpu.VMEM(proj_in_t.shape, bf16),
            pltpu.VMEM(proj_out_t.shape, bf16),
            pltpu.VMEM((tokens // wide, rank, wide), f32),
            pltpu.SemaphoreType.DMA((4,)),
        ],
    )


def fold_more(so_far, block, weight, slot, dtype):
    step, width = block.shape

    def body(f_ref, b_ref, w_ref, out_ref):
        share = lax.axis_index("tensor") ^ slot
        out_ref[...] = (f_ref[...] + fold_term(b_ref[...], w_ref, share)).astype(dtype)

    return call(
        body, arr((step, width), dtype), (so_far, block, near(weight)), 2 * step * width * width
    )


def halve(value):
    half = value.shape[0] // 2
    return value[:half] + value[half:]


def relay_shares(own, near_by, block, step, half):
    wide = own.shape[1]
    begin = block + step
    rank = wide // 2
    parts = half // wide

    def body(o_ref, n_ref, out_ref, keep_ref):
        row = lax.axis_index("tensor") // 2
        out_ref[:block, :] = o_ref[:block, :]
        out_ref[block : 2 * block, :] = n_ref[:block, :]
        u = o_ref[block:begin, :].astype(f32) + n_ref[block:begin, :].astype(f32)
        out_ref[2 * block : 2 * block + step, :] = split2(u[:, : wide // 2] + u[:, wide // 2 :], 1)
        for k in range(parts):
            mine, other = [
                o_ref[at, :].astype(f32) + n_ref[at, :].astype(f32)
                for at in [
                    pl.ds(pl.multiple_of(begin + (r * parts + k) * rank, rank), rank)
                    for r in (row, 1 - row)
                ]
            ]
            keep_ref[:, k * wide : (k + 1) * wide] = mine
            place = 2 * block + step + k * rank
            out_ref[place : place + rank, :] = other.astype(bf16)

    return call(
        body,
        (arr((2 * block + step + parts * rank, wide), bf16), arr((rank, half), f32)),
        (own, near_by),
    )


def first_logits(ours, theirs, mixed):
    step, width = ours.shape
    half = mixed.shape[0] // 2

    def body(a_ref, b_ref, m_ref, out_ref):
        weight = jnp.concatenate([a_ref[...], b_ref[...]], axis=0)
        row = 1 - lax.axis_index("tensor") // 2
        tokens = m_ref[pl.ds(pl.multiple_of(row * half, half), half), :]
        logits = lax.dot_general(weight, tokens, NT, preferred_element_type=f32)
        out_ref[...] = logits.astype(bf16)

    return call(
        body, arr((2 * step, half), bf16), (ours, theirs, mixed), 4 * step * half * width
    )


def gather_shares(own, cross, keep, block, step):
    wide = own.shape[1]
    parts = keep.shape[1] // wide
    begin = 2 * block

    def body(o_ref, c_ref, k_ref, out_ref, side_ref):
        me = lax.axis_index("tensor")
        for ref, share in ((o_ref, me), (c_ref, 3 - me)):
            for k, place in enumerate((share, share ^ 1)):
                place = pl.multiple_of(place * block, block)
                out_ref[pl.ds(place, block), :] = ref[k * block : (k + 1) * block, :]
        u = o_ref[begin : begin + step, :].astype(f32) + c_ref[begin : begin + step, :].astype(f32)
        out_ref[4 * block :, :] = split2(u[:, : wide // 2] + u[:, wide // 2 :], 1)
        for k in range(parts):
            cols = slice(k * wide, (k + 1) * wide)
            at = begin + step + k * (wide // 2)
            side_ref[:, cols] = k_ref[:, cols] + c_ref[at : at + wide // 2, :].astype(f32)

    return call(
        body,
        (arr((4 * block + step, wide), bf16), arr(keep.shape, f32)),
        (own, cross, keep),
        0,
    )


def pass_on(x):
    def body(x_ref, out_ref):
        out_ref[...] = x_ref[...]

    return call(body, arr(x.shape, x.dtype), (x,), 1 << 30)


def stack(pieces):
    high = pieces[0].shape[0]

    def body(*refs):
        for k, ref in enumerate(refs[:-1]):
            refs[-1][k * high : (k + 1) * high, :] = ref[...]

    return call(body, arr((high * len(pieces), pieces[0].shape[1]), bf16), tuple(pieces))


def logit_rows(folded, mixed, *after):
    slots = list(folded)
    step, width = folded[0].shape
    vocab = step * len(folded)
    half = mixed.shape[0] // 2

    def body(*refs):
        parts, refs = refs[: len(folded)], refs[len(folded) :]
        m_ref, (keep_ref, near_ref, other_ref, rest_ref) = refs[0], refs[-4:]
        row = lax.axis_index("tensor") // 2
        weight = jnp.concatenate([parts[slots.index(k)][...] for k in range(len(slots))], axis=0)
        tokens = m_ref[pl.ds(pl.multiple_of((1 - row) * half, half), half), :]
        other = lax.dot_general(weight, tokens, NT, preferred_element_type=f32).astype(bf16)
        other_ref[...] = other
        rest_ref[...] = other[2 * step :]
        tokens = m_ref[pl.ds(pl.multiple_of(row * half, half), half), :]
        mine = lax.dot_general(weight, tokens, NT, preferred_element_type=f32)
        keep_ref[...] = mine
        near_ref[...] = mine.astype(bf16)

    whole = (vocab, half)
    return call(
        body,
        (arr(whole, f32), arr(whole, bf16), arr(whole, bf16), arr((vocab - 2 * step, half), bf16)),
        (*folded.values(), mixed, *after),
        4 * vocab * half * width,
    )


def join(first, rest):
    high = first.shape[0]
    shape = (high + rest.shape[0], first.shape[1])

    def body(a_ref, b_ref, out_ref):
        out_ref[:high, :] = a_ref[...]
        out_ref[high:, :] = b_ref[...]

    return call(body, arr(shape, bf16), (first, rest), 1 << 30)


def token_grads(parts, pieces, side_in, targets, lengths):
    vocab, length = pieces[0].shape
    rank = side_in.shape[0]
    step = vocab // parts

    def body(k_ref, f_ref, c_ref, n_ref, side_ref, t_ref, live_ref, out_ref):
        row = lax.axis_index("tensor") // 2
        own = lax.axis_index("dp") % parts
        total = k_ref[...]
        for ref in (f_ref, c_ref, n_ref):
            total += ref[...].astype(f32)
        expo = jnp.exp(total)
        targets_here = jnp.where(row == 0, t_ref[0:1, :], t_ref[1:2, :])
        lengths_here = jnp.where(row == 0, live_ref[0:1, :], live_ref[1:2, :])
        live = lax.broadcasted_iota(jnp.int32, (1, length), 1) < lengths_here
        scale = jnp.where(live, 1.0 / jnp.sum(expo, axis=0, keepdims=True), 0.0)
        ids = lax.broadcasted_iota(jnp.int32, (vocab, length), 0) ^ (own * step)
        targets_here = jnp.where(live, targets_here, -1)
        grad = (expo * scale - jnp.where(ids == targets_here, 1.0, 0.0)).astype(bf16)
        joint = lax.dot_general(split2(side_ref[...], 0), grad, NT, preferred_element_type=f32)
        out_ref[...] = split2(halve(joint), 0)

    return call(
        body,
        arr((2 * rank, vocab), bf16),
        (*pieces, side_in, targets, lengths[:, None]),
        1 << 34,
    )


def row_scores(parts, joint, shares, queries):
    wide, vocab = joint.shape
    rank = wide // 2
    step = vocab // parts
    lines = rank // 2
    count = parts if queries is None else queries.shape[0]
    high = shares[0].shape[0] // 2
    rows = (high - step) // lines
    extra_args = () if queries is None else (queries,)

    def body(j_ref, a_ref, b_ref, c_ref, d_ref, *refs):
        q_ref, refs = (None, refs) if queries is None else (refs[0], refs[1:])
        out_ref, hold = refs
        own = lax.axis_index("dp") % parts
        s_refs = []
        for begin, pair in ((0, (a_ref, b_ref)), (1, (c_ref, d_ref)), (1, (a_ref, b_ref)), (0, (c_ref, d_ref))):
            s_refs += [ref.at[pl.ds(begin * high, high), :] for ref in pair]
        u = jnp.concatenate([ref[rows * lines :, :] for ref in s_refs], axis=0)
        grads = halve(jnp.dot(j_ref[...], u, preferred_element_type=f32))
        grads = grads[:, :rank] + grads[:, rank:]
        grads = jnp.concatenate([grads[:lines], grads[lines:]], axis=1)
        norm = jnp.sum(grads * grads, keepdims=True)
        low = grads.astype(bf16).astype(f32)
        for k in range(count):
            block = s_refs[k][: rows * lines, :] if q_ref is None else q_ref[k]
            terms = block.astype(f32).reshape(lines, rows, wide) * low[:, None, :]
            place = k if q_ref is not None else k ^ own
            at = pl.ds(pl.multiple_of(place * rows, rows), rows)
            hold[at, :] = split2(jnp.sum(terms, axis=0), 1)
        ones = jnp.ones((16, 2 * wide), bf16)
        inner = lax.dot_general(ones, hold[...], NT, preferred_element_type=f32)
        out_ref[...] = inner[:8] / jnp.sqrt(norm + eps)

    return call(
        body,
        arr((8, count * rows), f32),
        (joint, *shares, *extra_args),
        2 * vocab * rank * rank,
        scratch=[pltpu.VMEM((count * rows, 2 * wide), bf16)],
    )


def join_rows(own, crossed):
    def body(o_ref, c_ref, out_ref):
        first = lax.axis_index("tensor") < 2
        out_ref[0:1] = jnp.where(first, o_ref[0:1], c_ref[0:1])
        out_ref[1:2] = jnp.where(first, c_ref[0:1], o_ref[0:1])

    return call(body, arr(own.shape, f32), (own, crossed))


def pick_rows(joined, came):
    def body(j_ref, c_ref, out_ref):
        me = lax.axis_index("tensor")
        out_ref[...] = jnp.where((me == 1) | (me == 2), j_ref[0:2], c_ref[0:2])

    return call(body, arr((2, joined.shape[1]), f32), (joined, came))


def per_device(
    hidden, targets, lengths, conv_filter, proj_weight, unembed, proj_in, proj_out, query_grads
):
    rows = hidden.shape[0]
    n_dp, n_t = lax.axis_size("dp"), lax.axis_size("tensor")
    assert n_t == 4 and rows == 2
    parts = min(n_dp, 8)

    def send(x, pairs):
        return lax.ppermute(x, "tensor", pairs)

    def cross(x):
        pairs = [(d * 4 + a, e * 4 + b) for d in range(n_dp) for a, e, b in (
            (0, d ^ 1, 0), (1, d, 2), (2, d, 1), (3, d ^ 1, 3))]
        return lax.ppermute(x, ("dp", "tensor"), pairs)

    def swap(x, axis, slot):
        return lax.ppermute(x, axis, [(i, i ^ slot) for i in range(lax.axis_size(axis))])

    start = own_rows(parts, unembed)
    came = {s: swap(start, "tensor", s) for s in (2, 3, 1)}
    mixed, shares, folding, weight = local_work(
        hidden, conv_filter, proj_in.T, proj_out.T, query_grads, start, proj_weight
    )
    shares_near = send(shares, NEAR)
    for s in (2, 1, 3):
        folding = fold_more(folding, came[s], weight, s, bf16 if s == 3 else f32)
    block, step, half = query_grads.size // 128, start.shape[0], hidden.shape[1]
    across, keep_side = relay_shares(shares, shares_near, block, step, half)
    folded = {s: swap(folding, "dp", s) for s in reversed(range(2, parts, 2))}
    folded[0] = folding
    folded |= {s + 1: swap(x, "dp", 1) for s, x in folded.items()}
    first = pass_on(send(first_logits(folded[0], folded[1], mixed), FAR))
    whole, side_in = gather_shares(across, cross(across), keep_side, block, step)
    keep, near_logits, other_logits, rest = logit_rows(folded, mixed, side_in, first)
    far_logits = join(first, send(rest, FAR))
    pieces = (keep, far_logits, cross(other_logits), send(near_logits, NEAR))
    queries = None
    if n_dp != parts:
        queries = lax.all_gather(whole[: 4 * block], "dp", axis=0)
    others = {s: swap(whole, "dp", s) for s in range(2, parts, 2)}
    pairs = stack((whole, others[4])), stack((others[6], others[2]))
    shares = [y for x in pairs for y in (x, swap(x, "dp", 1))]
    joint = token_grads(parts, pieces, side_in, targets, lengths)
    scores = row_scores(parts, joint, shares, queries)
    joined = join_rows(scores, cross(scores))
    return pick_rows(joined, send(joined, NEAR))


def solution(mesh):
    in_specs = (
        P("dp", None, "tensor"),
        P("dp", None),
        P("dp"),
        P(None, "tensor"),
        P("tensor", None),
        P(None, "tensor"),
        P("tensor", None),
        P("tensor", None),
        P("dp", "tensor"),
    )
    return jax.shard_map(
        per_device, mesh=mesh, in_specs=in_specs, out_specs=P("dp", None), check_vma=False
    )
```

```python
import jax
import jax.numpy as jnp
from jax import lax
from jax.experimental import pallas as pl
from jax.experimental.pallas import tpu as pltpu
from jax.sharding import PartitionSpec as P

eps = 1e-06
f32, bf16 = jnp.float32, jnp.bfloat16
NT = (((1,), (1,)), ((), ()))
TN = (((0,), (0,)), ((), ()))
VM = pl.BlockSpec(memory_space=pltpu.VMEM)
ANY = pl.BlockSpec(memory_space=pl.ANY)
NEAR = [(0, 1), (1, 0), (2, 3), (3, 2)]
FAR = [(0, 2), (3, 1), (1, 0), (2, 3)]


def split2(value, axis):
    high = value.astype(bf16)
    low = (value - high.astype(f32)).astype(bf16)
    return jnp.concatenate([high, low], axis=axis)


def arr(shape, dtype):
    return jax.ShapeDtypeStruct(shape, dtype)


def call(body, outs, args, flops=0, in_specs=None, scratch=()):
    moved = sum(a.size * a.dtype.itemsize for a in args)
    return pl.pallas_call(
        body,
        out_shape=outs,
        in_specs=in_specs or [VM] * len(args),
        out_specs=jax.tree.map(lambda _: VM, outs),
        scratch_shapes=list(scratch),
        cost_estimate=pl.CostEstimate(flops=flops, bytes_accessed=moved, transcendentals=0),
        compiler_params=pltpu.CompilerParams(vmem_limit_bytes=32 << 20),
    )(*args)


def near(x):
    return pltpu.with_memory_space_constraint(x, pltpu.VMEM)


def far(x):
    return pltpu.with_memory_space_constraint(x, pltpu.HBM)


def own_rows(parts, unembed):
    vocab, width = unembed.shape
    step = vocab // parts

    def body(e_ref, out_ref, sem):
        own = pl.multiple_of((lax.axis_index("dp") % parts) * step, step)
        copy = pltpu.make_async_copy(e_ref.at[pl.ds(own, step), :], out_ref, sem)
        copy.start()
        copy.wait()

    return call(
        body,
        arr((step, width), bf16),
        (far(unembed),),
        in_specs=[ANY],
        scratch=[pltpu.SemaphoreType.DMA],
    )


def fold_term(rows, w_ref, share):
    width = rows.shape[1]
    cols = pl.ds(pl.multiple_of(share * width, width), width)
    return lax.dot_general(rows, w_ref[:, cols], NT, preferred_element_type=f32)


def local_work(hidden, conv_filter, proj_in_t, proj_out_t, query_grads, start, proj_weight):
    rows, length, width = hidden.shape
    rank = proj_in_t.shape[0]
    step = start.shape[0]
    tokens = rows * length
    wide = 2 * rank
    q_rows = query_grads.shape[0]
    lines = width // wide
    u_begin = lines * q_rows
    side_begin = u_begin + step

    def body(
        h_any, p_any, o_any, q_any, w_any, c_ref, b_ref,
        mixed_ref, out_ref, fold_ref, w_ref, h_ref, p_ref, o_ref, q_ref, hold, sems,
    ):
        pairs = ((h_any, h_ref), (p_any, p_ref), (o_any, o_ref), (q_any, q_ref), (w_any, w_ref))
        copies = [pltpu.make_async_copy(a, b, sems.at[k]) for k, (a, b) in enumerate(pairs)]
        for copy in copies:
            copy.start()
        taps = c_ref[...].astype(f32)
        place = lax.broadcasted_iota(jnp.int32, (length, width), 0)
        copies[0].wait()
        for row in range(rows):
            here = h_ref[row].astype(f32)
            first = jnp.where(place >= 1, pltpu.roll(here, 1, 0), 0.0)
            second = jnp.where(place >= 2, pltpu.roll(here, 2, 0), 0.0)
            mixed_ref[pl.ds(row * length, length), :] = (
                taps[0:1] * here + taps[1:2] * first + taps[2:3] * second
            ).astype(bf16)
        copies[1].wait()
        side = lax.dot_general(p_ref[...], mixed_ref[...], NT, preferred_element_type=f32)
        for k in range(tokens // wide):
            hold[k] = side[:, k * wide : (k + 1) * wide]
        for k in range(tokens // wide):
            pair = [hold[k, pl.ds(odd, rank // 2, stride=2), :] for odd in (0, 1)]
            begin = side_begin + k * rank
            out_ref[begin : begin + rank, :] = jnp.concatenate(pair, axis=0).astype(bf16)
        copies[3].wait()
        for k in range(lines):
            out_ref[k * q_rows : (k + 1) * q_rows, :] = q_ref[:, k * wide : (k + 1) * wide]
        copies[2].wait()
        u = lax.dot_general(b_ref[...], o_ref[...], NT, preferred_element_type=f32)
        out_ref[u_begin:side_begin, :] = split2(u, 1)
        copies[4].wait()
        fold_ref[...] = fold_term(b_ref[...], w_ref, lax.axis_index("tensor"))

    return call(
        body,
        (
            arr((tokens, width), bf16),
            arr((side_begin + tokens // wide * rank, wide), bf16),
            arr((step, width), f32),
            pltpu.VMEM(proj_weight.shape, bf16),
        ),
        (*(far(x) for x in (hidden, proj_in_t, proj_out_t, query_grads, proj_weight)), conv_filter, start),
        2 * tokens * width * rank + 2 * step * width * width,
        in_specs=[ANY] * 5 + [VM] * 2,
        scratch=[
            pltpu.VMEM(hidden.shape, bf16),
            pltpu.VMEM(proj_in_t.shape, bf16),
            pltpu.VMEM(proj_out_t.shape, bf16),
            pltpu.VMEM(query_grads.shape, bf16),
            pltpu.VMEM((tokens // wide, rank, wide), f32),
            pltpu.SemaphoreType.DMA((5,)),
        ],
    )


def fold_more(so_far, block, weight, slot, dtype):
    step, width = block.shape

    def body(f_ref, b_ref, w_ref, out_ref):
        share = lax.axis_index("tensor") ^ slot
        out_ref[...] = (f_ref[...] + fold_term(b_ref[...], w_ref, share)).astype(dtype)

    return call(
        body, arr((step, width), dtype), (so_far, block, near(weight)), 2 * step * width * width
    )


def halve(value):
    half = value.shape[0] // 2
    return value[:half] + value[half:]


def relay_shares(own, near_by, block, step, half):
    wide = own.shape[1]
    begin = block + step
    rank = wide // 2
    parts = half // wide

    def body(o_ref, n_ref, out_ref, keep_ref):
        row = lax.axis_index("tensor") // 2
        out_ref[:block, :] = o_ref[:block, :]
        out_ref[block : 2 * block, :] = n_ref[:block, :]
        u = o_ref[block:begin, :].astype(f32) + n_ref[block:begin, :].astype(f32)
        out_ref[2 * block : 2 * block + step, :] = split2(u[:, : wide // 2] + u[:, wide // 2 :], 1)
        for k in range(parts):
            mine, other = [
                o_ref[at, :].astype(f32) + n_ref[at, :].astype(f32)
                for at in [
                    pl.ds(pl.multiple_of(begin + (r * parts + k) * rank, rank), rank)
                    for r in (row, 1 - row)
                ]
            ]
            keep_ref[:, k * wide : (k + 1) * wide] = mine
            place = 2 * block + step + k * rank
            out_ref[place : place + rank, :] = other.astype(bf16)

    return call(
        body,
        (arr((2 * block + step + parts * rank, wide), bf16), arr((rank, half), f32)),
        (own, near_by),
    )


def first_logits(ours, theirs, mixed):
    step, width = ours.shape
    half = mixed.shape[0] // 2

    def body(a_ref, b_ref, m_ref, out_ref):
        weight = jnp.concatenate([a_ref[...], b_ref[...]], axis=0)
        row = 1 - lax.axis_index("tensor") // 2
        tokens = m_ref[pl.ds(pl.multiple_of(row * half, half), half), :]
        logits = lax.dot_general(weight, tokens, NT, preferred_element_type=f32)
        out_ref[...] = logits.astype(bf16)

    return call(
        body, arr((2 * step, half), bf16), (ours, theirs, mixed), 4 * step * half * width
    )


def gather_shares(own, cross, keep, block, step):
    wide = own.shape[1]
    parts = keep.shape[1] // wide
    begin = 2 * block

    def body(o_ref, c_ref, k_ref, out_ref, side_ref):
        me = lax.axis_index("tensor")
        for ref, share in ((o_ref, me), (c_ref, 3 - me)):
            for k, place in enumerate((share, share ^ 1)):
                place = pl.multiple_of(place * block, block)
                out_ref[pl.ds(place, block), :] = ref[k * block : (k + 1) * block, :]
        u = o_ref[begin : begin + step, :].astype(f32) + c_ref[begin : begin + step, :].astype(f32)
        out_ref[4 * block :, :] = split2(u[:, : wide // 2] + u[:, wide // 2 :], 1)
        for k in range(parts):
            cols = slice(k * wide, (k + 1) * wide)
            at = begin + step + k * (wide // 2)
            side_ref[:, cols] = k_ref[:, cols] + c_ref[at : at + wide // 2, :].astype(f32)

    return call(
        body,
        (arr((4 * block + step, wide), bf16), arr(keep.shape, f32)),
        (own, cross, keep),
        0,
    )


def pass_on(x):
    def body(x_ref, out_ref):
        out_ref[...] = x_ref[...]

    return call(body, arr(x.shape, x.dtype), (x,), 1 << 30)


def stack(pieces):
    high = pieces[0].shape[0]

    def body(*refs):
        for k, ref in enumerate(refs[:-1]):
            refs[-1][k * high : (k + 1) * high, :] = ref[...]

    return call(body, arr((high * len(pieces), pieces[0].shape[1]), bf16), tuple(pieces))


def logit_rows(folded, mixed, *after):
    slots = list(folded)
    step, width = folded[0].shape
    vocab = step * len(folded)
    half = mixed.shape[0] // 2

    def body(*refs):
        parts, refs = refs[: len(folded)], refs[len(folded) :]
        m_ref, (keep_ref, near_ref, other_ref, rest_ref) = refs[0], refs[-4:]
        row = lax.axis_index("tensor") // 2
        weight = jnp.concatenate([parts[slots.index(k)][...] for k in range(len(slots))], axis=0)
        tokens = m_ref[pl.ds(pl.multiple_of((1 - row) * half, half), half), :]
        other = lax.dot_general(weight, tokens, NT, preferred_element_type=f32).astype(bf16)
        other_ref[...] = other
        rest_ref[...] = other[2 * step :]
        tokens = m_ref[pl.ds(pl.multiple_of(row * half, half), half), :]
        mine = lax.dot_general(weight, tokens, NT, preferred_element_type=f32)
        keep_ref[...] = mine
        near_ref[...] = mine.astype(bf16)

    whole = (vocab, half)
    return call(
        body,
        (arr(whole, f32), arr(whole, bf16), arr(whole, bf16), arr((vocab - 2 * step, half), bf16)),
        (*folded.values(), mixed, *after),
        4 * vocab * half * width,
    )


def token_grads(parts, pieces, first, side_in, targets, lengths):
    vocab, length = pieces[0].shape
    rank = side_in.shape[0]
    step = vocab // parts

    def body(k_ref, n_ref, c_ref, f_ref, l_ref, side_ref, t_ref, live_ref, out_ref):
        row = lax.axis_index("tensor") // 2
        own = lax.axis_index("dp") % parts
        total = k_ref[...] + n_ref[...].astype(f32) + c_ref[...].astype(f32)
        total += jnp.concatenate([l_ref[...], f_ref[...]], axis=0).astype(f32)
        expo = jnp.exp(total)
        targets_here = jnp.where(row == 0, t_ref[0:1, :], t_ref[1:2, :])
        lengths_here = jnp.where(row == 0, live_ref[0:1, :], live_ref[1:2, :])
        live = lax.broadcasted_iota(jnp.int32, (1, length), 1) < lengths_here
        scale = jnp.where(live, 1.0 / jnp.sum(expo, axis=0, keepdims=True), 0.0)
        ids = lax.broadcasted_iota(jnp.int32, (vocab, length), 0) ^ (own * step)
        targets_here = jnp.where(live, targets_here, -1)
        grad = (expo * scale - jnp.where(ids == targets_here, 1.0, 0.0)).astype(bf16)
        joint = lax.dot_general(split2(side_ref[...], 0), grad, NT, preferred_element_type=f32)
        out_ref[...] = split2(halve(joint), 0)

    return call(
        body,
        arr((2 * rank, vocab), bf16),
        (*pieces, first, side_in, targets, lengths[:, None]),
        1 << 34,
    )


def row_scores(parts, joint, shares, queries):
    wide, vocab = joint.shape
    rank = wide // 2
    step = vocab // parts
    lines = rank // 2
    count = parts if queries is None else queries.shape[0]
    high = shares[2].shape[0]
    rows = (high - step) // lines
    extra_args = () if queries is None else (queries,)

    def body(j_ref, a_ref, b_ref, c_ref, d_ref, *refs):
        q_ref, refs = (None, refs) if queries is None else (refs[0], refs[1:])
        out_ref, hold = refs
        own = lax.axis_index("dp") % parts
        cut = [[ref.at[pl.ds(k * high, high), :] for ref in (a_ref, b_ref)] for k in range(3)]
        s_refs = [*cut[0], c_ref, d_ref, *cut[1], *cut[2]]
        u = jnp.concatenate([ref[rows * lines :, :] for ref in s_refs], axis=0)
        grads = halve(jnp.dot(j_ref[...], u, preferred_element_type=f32))
        grads = grads[:, :rank] + grads[:, rank:]
        grads = jnp.concatenate([grads[:lines], grads[lines:]], axis=1)
        norm = jnp.sum(grads * grads, keepdims=True)
        low = grads.astype(bf16).astype(f32)
        for k in range(count):
            block = s_refs[k][: rows * lines, :] if q_ref is None else q_ref[k]
            terms = block.astype(f32).reshape(lines, rows, wide) * low[:, None, :]
            place = k if q_ref is not None else k ^ own
            at = pl.ds(pl.multiple_of(place * rows, rows), rows)
            hold[at, :] = split2(jnp.sum(terms, axis=0), 1)
        ones = jnp.ones((16, 2 * wide), bf16)
        inner = lax.dot_general(ones, hold[...], NT, preferred_element_type=f32)
        out_ref[...] = inner[:8] / jnp.sqrt(norm + eps)

    return call(
        body,
        arr((8, count * rows), f32),
        (joint, *shares, *extra_args),
        2 * vocab * rank * rank,
        scratch=[pltpu.VMEM((count * rows, 2 * wide), bf16)],
    )


def join_rows(own, crossed):
    def body(o_ref, c_ref, out_ref):
        first = lax.axis_index("tensor") < 2
        out_ref[0:1] = jnp.where(first, o_ref[0:1], c_ref[0:1])
        out_ref[1:2] = jnp.where(first, c_ref[0:1], o_ref[0:1])

    return call(body, arr(own.shape, f32), (own, crossed))


def pick_rows(joined, came):
    def body(j_ref, c_ref, out_ref):
        me = lax.axis_index("tensor")
        out_ref[...] = jnp.where((me == 1) | (me == 2), j_ref[0:2], c_ref[0:2])

    return call(body, arr((2, joined.shape[1]), f32), (joined, came))


def per_device(
    hidden, targets, lengths, conv_filter, proj_weight, unembed, proj_in, proj_out, query_grads
):
    rows = hidden.shape[0]
    n_dp, n_t = lax.axis_size("dp"), lax.axis_size("tensor")
    assert n_t == 4 and rows == 2
    parts = min(n_dp, 8)

    def send(x, pairs):
        return lax.ppermute(x, "tensor", pairs)

    def cross(x):
        pairs = [(d * 4 + a, e * 4 + b) for d in range(n_dp) for a, e, b in (
            (0, d ^ 1, 0), (1, d, 2), (2, d, 1), (3, d ^ 1, 3))]
        return lax.ppermute(x, ("dp", "tensor"), pairs)

    def swap(x, axis, slot):
        return lax.ppermute(x, axis, [(i, i ^ slot) for i in range(lax.axis_size(axis))])

    start = own_rows(parts, unembed)
    came = {s: swap(start, "tensor", s) for s in (2, 3, 1)}
    mixed, shares, folding, weight = local_work(
        hidden, conv_filter, proj_in.T, proj_out.T, query_grads, start, proj_weight
    )
    shares_near = send(shares, NEAR)
    for s in (2, 1, 3):
        folding = fold_more(folding, came[s], weight, s, bf16 if s == 3 else f32)
    block, step, half = query_grads.size // 128, start.shape[0], hidden.shape[1]
    across, keep_side = relay_shares(shares, shares_near, block, step, half)
    folded = {s: swap(folding, "dp", s) for s in reversed(range(2, parts, 2))}
    folded[0] = folding
    folded |= {s + 1: swap(x, "dp", 1) for s, x in folded.items()}
    first = pass_on(send(first_logits(folded[0], folded[1], mixed), FAR))
    whole, side_in = gather_shares(across, cross(across), keep_side, block, step)
    keep, near_logits, other_logits, rest = logit_rows(folded, mixed, side_in, first)
    pieces = (keep, send(near_logits, NEAR), cross(other_logits), send(rest, FAR))
    queries = None
    if n_dp != parts:
        queries = lax.all_gather(whole[: 4 * block], "dp", axis=0)
    others = {s: swap(whole, "dp", s) for s in range(2, parts, 2)}
    first_three = stack((whole, others[4], others[6]))
    shares = [y for x in (first_three, others[2]) for y in (x, swap(x, "dp", 1))]
    joint = token_grads(parts, pieces, first, side_in, targets, lengths)
    scores = row_scores(parts, joint, shares, queries)
    joined = join_rows(scores, cross(scores))
    return pick_rows(joined, send(joined, NEAR))


def solution(mesh):
    in_specs = (
        P("dp", None, "tensor"),
        P("dp", None),
        P("dp"),
        P(None, "tensor"),
        P("tensor", None),
        P(None, "tensor"),
        P("tensor", None),
        P("tensor", None),
        P("dp", "tensor"),
    )
    return jax.shard_map(
        per_device, mesh=mesh, in_specs=in_specs, out_specs=P("dp", None), check_vma=False
    )
```
